256 devices in a mesh: wide: 64 (over y, z_hi, x, core), narrow: 4 (over z_lo).
Axes of the slice: x: 4, y: 4, z: 8 (z_hi: 2, z_lo: 4; z = z_hi * 4 + z_lo), core: 2. Of those that a mesh axis runs over, the one named last changes fastest.
Arguments:
- image_raw: float32 [12288, 1152], P(('wide', 'narrow')), may hold values from -3 to 3
- text_raw: float32 [12288, 1152], P(('wide', 'narrow')), may hold values from -3 to 3
- image_ids: int32 [12288], replicated, may hold values from 0 to 3071, as said below
- text_ids: int32 [12288], replicated, may hold values from 0 to 3071, as said below
- log_temp: float32 [1], replicated, may hold values from 2.3 to 3.7
- bias: float32 [1], replicated, may hold values from -12 to -8
Outputs:
- loss: float32 [1], replicated
- image_grad: float32 [12288, 1152], P(('wide', 'narrow'))
- text_grad: float32 [12288, 1152], P(('wide', 'narrow'))
- temp_grad: float32 [1], replicated
- bias_grad: float32 [1], replicated
The draws below stay inside these ranges and needn't reach their ends.
Inputs may be any that keep to these rules, and one draw needn't show every extreme that they name: `image_ids`: each pair id names exactly 4 images. `text_ids`: each pair id names exactly 4 texts; a text and an image with the same id form a positive pair.
All inputs are finite; a program needn't handle non-finite values.
Results may differ from the reference program's by a relative error of at most 0.0029.
Values may be sent and summed in bfloat16 or wider, within the bound.
No kernel may reach another device: no remote copies, remote signals or barrier semaphores. Data moves between devices by JAX's collectives and lax.ppermute only.
A program may use at most 128 MiB of HBM per device.

```python
import math
import jax
import jax.numpy as jnp
from jax import lax

D = 1152
B = 12288


def pair_layout(key):
    image_order = jax.random.permutation(jax.random.fold_in(key, 11), B)
    text_order = jax.random.permutation(jax.random.fold_in(key, 12), B)
    return ((image_order // 4).astype(jnp.int32), (text_order // 4).astype(jnp.int32))


def shared_latent(key, ids, spread):
    groups = max(B // 64, 1)
    centres = jax.random.truncated_normal(jax.random.fold_in(key, 13), -4.0, 4.0, (groups, D), jnp.float32)
    own_part = jax.random.truncated_normal(jax.random.fold_in(key, 14), -4.0, 4.0, (B // 4, D), jnp.float32)
    group_of = (ids % groups).astype(jnp.int32)
    return spread * jnp.take(centres, group_of, axis=0) + jnp.take(own_part, ids, axis=0)


def build_rows(key, latent, noise, scale_top):
    amplitude = jax.random.uniform(jax.random.fold_in(key, 1), (B, 1), jnp.float32, 0.4, 1.3)
    row_scale = jnp.exp(jax.random.uniform(jax.random.fold_in(key, 2), (B, 1), jnp.float32, 0.0, math.log(scale_top)))
    return 0.03 * row_scale * (amplitude * latent + noise)


def draw_image_raw(key, part):
    own_key = jax.random.fold_in(key, 21)
    image_ids, text_ids = pair_layout(key)
    latent = shared_latent(key, image_ids, 0.7)
    noise = jax.random.truncated_normal(jax.random.fold_in(own_key, 3), -4.0, 4.0, (B, D), jnp.float32)
    return build_rows(own_key, latent, noise, 1.0)


def draw_text_raw(key, part):
    own_key = jax.random.fold_in(key, 22)
    image_ids, text_ids = pair_layout(key)
    latent = shared_latent(key, text_ids, 0.7)
    noise = jax.random.truncated_normal(jax.random.fold_in(own_key, 3), -4.0, 4.0, (B, D), jnp.float32)
    return build_rows(own_key, latent, noise, 1.0)


def draw_image_ids(key, part):
    image_ids, text_ids = pair_layout(key)
    return image_ids


def draw_text_ids(key, part):
    image_ids, text_ids = pair_layout(key)
    return text_ids


def setup_inputs(seed: int = 0) -> dict:
    streams_of = jax.random.split(jax.random.key(seed), 7)
    image_raw = draw_image_raw(jax.random.fold_in(streams_of[6], 71), 0)
    text_raw = draw_text_raw(jax.random.fold_in(streams_of[6], 71), 0)
    image_ids = draw_image_ids(jax.random.fold_in(streams_of[6], 71), 0)
    text_ids = draw_text_ids(jax.random.fold_in(streams_of[6], 71), 0)
    log_temp = jnp.clip(jax.random.uniform(streams_of[4], (1,), jnp.float32, 2.3, 3.7), 2.3, 3.7)
    bias = jnp.clip(jax.random.uniform(streams_of[5], (1,), jnp.float32, -12.0, -8.0), -12.0, -8.0)
    return {"image_raw": image_raw, "text_raw": text_raw, "image_ids": image_ids, "text_ids": text_ids, "log_temp": log_temp, "bias": bias}


def unit(rows):
    scale = jnp.sqrt(lax.optimization_barrier(jnp.mean(rows * rows, axis=-1, keepdims=True)) + 1e-06)
    return rows / (scale * math.sqrt(rows.shape[-1]))

def reference(image_raw, text_raw, image_ids, text_ids, log_temp, bias):
    total = image_raw.shape[0]
    width = image_raw.shape[1]
    image_float, image_back = jax.vjp(unit, image_raw)
    text_float, text_back = jax.vjp(unit, text_raw)
    image_unit = image_float.astype(jnp.bfloat16)
    text_unit = text_float.astype(jnp.bfloat16)
    temp = jnp.exp(log_temp[0])
    offset = bias[0]
    block = math.gcd(total, 512)
    count = total // block

    def step(carry, inputs):
        image_acc, loss_acc, bias_acc, temp_acc = carry
        rows, ids = inputs
        cosine = jnp.dot(rows, image_unit.T, preferred_element_type=jnp.float32)
        logits = temp * cosine + offset
        label = jnp.where(ids[:, None] == image_ids[None, :], 1.0, -1.0).astype(jnp.float32)
        loss_acc = loss_acc + jnp.sum(jax.nn.softplus(-label * logits)) / total
        scaled = -label * jax.nn.sigmoid(-label * logits)
        bias_acc = bias_acc + jnp.sum(scaled) / total
        temp_acc = temp_acc + jnp.sum(scaled * temp * cosine) / total
        scaled_low = scaled.astype(jnp.bfloat16)
        text_part = temp * jnp.dot(scaled_low, image_unit, preferred_element_type=jnp.float32)
        image_acc = image_acc + temp * jnp.dot(scaled_low.T, rows, preferred_element_type=jnp.float32)
        return ((image_acc, loss_acc, bias_acc, temp_acc), text_part)
    start = (jnp.zeros((total, width), jnp.float32), jnp.zeros((), jnp.float32), jnp.zeros((), jnp.float32), jnp.zeros((), jnp.float32))
    carry, text_parts = lax.scan(step, start, (text_unit.reshape(count, block, width), text_ids.reshape(count, block)))
    image_acc, loss_acc, bias_acc, temp_acc = carry
    text_unit_grad = text_parts.reshape(total, width)
    image_grad = image_back(image_acc)[0]
    text_grad = text_back(text_unit_grad)[0]
    return (loss_acc.reshape(1), image_grad, text_grad, temp_acc.reshape(1), bias_acc.reshape(1))
```

```python
import math

import jax
import jax.numpy as jnp
import numpy as np
from jax import lax
from jax.experimental import pallas as pl
from jax.experimental.pallas import tpu as pltpu
from jax.sharding import Mesh
from jax.sharding import PartitionSpec as P

SIZES = (4, 2, 4, 2, 4)
AXES = ("y", "zh", "x", "core", "zl")
ROWS = 48
OFFSETS = (1, 3, 2)
ZOFFSETS = (2, 6, 4)
VMEM = pl.BlockSpec(memory_space=pltpu.VMEM)
SMEM = pl.BlockSpec(memory_space=pltpu.SMEM)


def flat(x, y, z, c):
    return (((y * 2 + z // 4) * 4 + x) * 2 + c) * 4 + z % 4


def send(value, where):
    pairs = []
    for y, zh, x, c, zl in np.ndindex(*SIZES):
        z = zh * 4 + zl
        tx, ty, tz, tc = where(x, y, z, c)
        pairs.append((flat(x, y, z, c), flat(tx % 4, ty % 4, tz % 8, tc % 2)))
    return lax.ppermute(value, AXES, pairs)


def along_first(k):
    return lambda x, y, z, c: (x + k, y, z, c) if c == 0 else (x, y + k, z, c)


def along_second(k):
    return lambda x, y, z, c: (x, y + k, z, c) if c == 0 else (x + k, y, z, c)


def along_z(k):
    return lambda x, y, z, c: (x, y, z + k, c)


def pair_up(sign):
    return lambda x, y, z, c: (x, y, z + sign, c) if c == 0 else (x, y, z - sign, c)


def swap(x, y, z, c):
    return (x, y, z, 1 - c)


def unit_kernel(image_ref, text_ref, image_out, text_out):
    for src, dst in ((image_ref, image_out), (text_ref, text_out)):
        rows = src[...]
        scale = jnp.sqrt(jnp.mean(rows * rows, axis=-1, keepdims=True) + 1e-06)
        dst[...] = (rows / (scale * math.sqrt(rows.shape[-1]))).astype(jnp.bfloat16)


def grid_kernel(
    scalars, rows_id, cols_id, t0, t1, i0, i1, i2, i3,
    text_own, text_other, image_own, image_1, image_2, image_3, sums,
    text, image, scaled,
):
    temp = scalars[0]
    offset = scalars[1]
    for n, src in enumerate((t0, t1)):
        text[384 * n : 384 * (n + 1), :] = src[...]
    for n, src in enumerate((i0, i1, i2, i3)):
        image[192 * n : 192 * (n + 1), :] = src[...]
    cols = cols_id[...]
    totals = [jnp.zeros((8, 768), jnp.float32)] * 3
    for tile in range(3):
        at = slice(256 * tile, 256 * (tile + 1))
        cosine = lax.dot_general(
            text[at, :], image[...], (((1,), (1,)), ((), ())), preferred_element_type=jnp.float32
        )
        logits = temp * cosine + offset
        same = rows_id[at, :] == cols
        margin = jnp.where(same, -logits, logits)
        decay = jnp.exp(-jnp.abs(margin))
        inverse = 1.0 / (1.0 + decay)
        sigmoid = jnp.where(margin >= 0, inverse, decay * inverse)
        grad = jnp.where(same, -sigmoid, sigmoid)
        loss = jnp.maximum(margin, 0.0) + jnp.log1p(decay)
        scaled[at, :] = grad.astype(jnp.bfloat16)
        for n, value in enumerate((loss, grad, grad * cosine)):
            totals[n] = totals[n] + jnp.sum(value.reshape(32, 8, 768), axis=0)
    lane = lax.broadcasted_iota(jnp.int32, (8, 128), 1)
    out = jnp.zeros((8, 128), jnp.float32)
    for n in range(3):
        out = jnp.where(lane == n, jnp.sum(totals[n]), out)
    sums[...] = out
    for tile in range(3):
        at = slice(256 * tile, 256 * (tile + 1))
        part = jnp.dot(scaled[at, :], image[...], preferred_element_type=jnp.float32)
        for n in range(2):
            low, high = max(256 * tile, 384 * n), min(256 * (tile + 1), 384 * (n + 1))
            if low < high:
                piece = part[low - 256 * tile : high - 256 * tile, :]
                dst = (text_own, text_other)[n]
                dst[low - 384 * n : high - 384 * n, :] = piece.astype(dst.dtype)
    for n, dst in enumerate((image_own, image_1, image_2, image_3)):
        part = lax.dot_general(
            scaled[:, 192 * n : 192 * (n + 1)], text[...], (((0,), (0,)), ((), ())),
            preferred_element_type=jnp.float32,
        )
        dst[...] = part.astype(dst.dtype)


def finish_kernel(scalars, raw, own, r1, r2, r3, out):
    rows = raw[...]
    width = rows.shape[-1]
    grad = own[...] + r1[...].astype(jnp.float32) + r2[...].astype(jnp.float32) + r3[...].astype(jnp.float32)
    grad = grad * scalars[0]
    square = jnp.mean(rows * rows, axis=-1, keepdims=True) + 1e-06
    inner = jnp.sum(rows * grad, axis=-1, keepdims=True)
    out[...] = (grad - rows * (inner / (square * width))) / (jnp.sqrt(square) * math.sqrt(width))


def f32(*shape):
    return jax.ShapeDtypeStruct(shape, jnp.float32)


def b16(*shape):
    return jax.ShapeDtypeStruct(shape, jnp.bfloat16)


def body(image_raw, text_raw, image_ids, text_ids, log_temp, bias):
    pairs, width = image_raw.shape
    total = pairs * 256
    x, y, c = lax.axis_index("x"), lax.axis_index("y"), lax.axis_index("core")
    z = lax.axis_index("zh") * 4 + lax.axis_index("zl")
    image_unit, text_unit = pl.pallas_call(
        unit_kernel,
        out_shape=(b16(pairs, width), b16(pairs, width)),
        in_specs=[VMEM] * 2,
        out_specs=(VMEM, VMEM),
    )(image_raw, text_raw)

    line = [image_unit] + [send(image_unit, along_first(k)) for k in OFFSETS]
    ring = [text_unit] + [send(text_unit, along_z(k)) for k in ZOFFSETS]
    line = jnp.concatenate(line, 0)
    ring = jnp.concatenate(ring, 0)
    ring_next = send(ring, pair_up(1))
    plane = [line] + [send(line, along_second(k)) for k in OFFSETS]
    column = jnp.concatenate([ring, ring_next], 0)
    column_other = send(column, swap)

    back = (0,) + OFFSETS
    zback = (0,) + ZOFFSETS
    cols_from = []
    for k in back:
        for j in back:
            sx = jnp.where(c == 0, x - j, x - k) % 4
            sy = jnp.where(c == 0, y - k, y - j) % 4
            cols_from.append(flat(sx, sy, z, c))
    rows_from = []
    for core in (c, 1 - c):
        for step in (0, 1):
            start = z + jnp.where(core == 0, -step, step)
            for k in zback:
                rows_from.append(flat(x, y, (start - k) % 8, core))
    cols_id = image_ids.reshape(256, pairs)[jnp.stack(cols_from)].reshape(1, 16 * pairs)
    rows_id = text_ids.reshape(256, pairs)[jnp.stack(rows_from)].reshape(16 * pairs, 1)

    temp = jnp.exp(log_temp[0])
    scalars = jnp.stack([temp, bias[0]])
    text_own, text_far, image_own, image_1, image_2, image_3, sums = pl.pallas_call(
        grid_kernel,
        out_shape=(
            f32(384, width), b16(384, width), f32(192, width), b16(192, width), b16(192, width), b16(192, width),
            f32(8, 128),
        ),
        in_specs=[SMEM] + [VMEM] * 8,
        out_specs=(VMEM,) * 7,
        scratch_shapes=[
            pltpu.VMEM((768, width), jnp.bfloat16),
            pltpu.VMEM((768, width), jnp.bfloat16),
            pltpu.VMEM((768, 768), jnp.bfloat16),
        ],
        compiler_params=pltpu.CompilerParams(vmem_limit_bytes=48 * 1024 * 1024),
    )(scalars, rows_id, cols_id, column, column_other, *plane)

    text_sum = text_own + send(text_far, swap).astype(jnp.float32)
    image_parts = [send(p, along_second(-k)) for p, k in zip((image_1, image_2, image_3), OFFSETS)]
    near = text_sum[:192] + send(text_sum[192:].astype(jnp.bfloat16), pair_up(-1)).astype(jnp.float32)
    image_sum = image_own + sum(p.astype(jnp.float32) for p in image_parts)
    near_low = near.astype(jnp.bfloat16)
    image_low = image_sum.astype(jnp.bfloat16)
    text_parts = [send(near_low[48 * n : 48 * n + 48], along_z(-k)) for n, k in enumerate(ZOFFSETS, 1)]
    image_parts = [send(image_low[48 * n : 48 * n + 48], along_first(-k)) for n, k in enumerate(OFFSETS, 1)]

    for where in (
        swap, along_z(1), along_z(2), along_z(4), along_first(1), along_first(2), along_second(1), along_second(2),
    ):
        sums = sums + send(sums, where)

    finish = pl.pallas_call(
        finish_kernel,
        out_shape=f32(pairs, width),
        in_specs=[SMEM] + [VMEM] * 5,
        out_specs=VMEM,
    )
    image_grad = finish(scalars, image_raw, image_sum[:48], *image_parts)
    text_grad = finish(scalars, text_raw, near[:48], *text_parts)
    return (sums[0, 0:1] / total, image_grad, text_grad, sums[0, 2:3] * temp / total, sums[0, 1:2] / total)


def solution(mesh):
    fine = Mesh(mesh.devices.reshape(SIZES), AXES)
    rows = P(AXES, None)
    return jax.shard_map(
        body,
        mesh=fine,
        in_specs=(rows, rows, P(), P(), P(), P()),
        out_specs=(P(), rows, rows, P(), P()),
        check_vma=False,
    )
```

```python
import math

import jax
import jax.numpy as jnp
import numpy as np
from jax import lax
from jax.experimental import pallas as pl
from jax.experimental.pallas import tpu as pltpu
from jax.sharding import Mesh
from jax.sharding import PartitionSpec as P

SIZES = (4, 2, 4, 2, 4)
AXES = ("y", "zh", "x", "core", "zl")
ROWS = 48
OFFSETS = (1, 3, 2)
ZOFFSETS = (2, 6, 4)
VMEM = pl.BlockSpec(memory_space=pltpu.VMEM)
SMEM = pl.BlockSpec(memory_space=pltpu.SMEM)


def flat(x, y, z, c):
    return (((y * 2 + z // 4) * 4 + x) * 2 + c) * 4 + z % 4


def send(value, where, name="move"):
    pairs = []
    for y, zh, x, c, zl in np.ndindex(*SIZES):
        z = zh * 4 + zl
        tx, ty, tz, tc = where(x, y, z, c)
        pairs.append((flat(x, y, z, c), flat(tx % 4, ty % 4, tz % 8, tc % 2)))
    with jax.named_scope(name):
        return lax.ppermute(value, AXES, pairs)


def along_first(k):
    return lambda x, y, z, c: (x + k, y, z, c) if c == 0 else (x, y + k, z, c)


def along_second(k):
    return lambda x, y, z, c: (x, y + k, z, c) if c == 0 else (x + k, y, z, c)


def along_z(k):
    return lambda x, y, z, c: (x, y, z + k, c)


def pair_up(sign):
    return lambda x, y, z, c: (x, y, z + sign, c) if c == 0 else (x, y, z - sign, c)


def swap(x, y, z, c):
    return (x, y, z, 1 - c)


def unit_kernel(image_ref, text_ref, image_out, text_out):
    for src, dst in ((image_ref, image_out), (text_ref, text_out)):
        rows = src[...]
        scale = jnp.sqrt(jnp.mean(rows * rows, axis=-1, keepdims=True) + 1e-06)
        dst[...] = (rows / (scale * math.sqrt(rows.shape[-1]))).astype(jnp.bfloat16)


def join_kernel(*refs):
    *sources, out = refs
    rows = sources[0].shape[0]
    for n, src in enumerate(sources):
        out[rows * n : rows * (n + 1), :] = src[...]


def join(*pieces):
    rows, width = pieces[0].shape
    return pl.pallas_call(
        join_kernel,
        out_shape=b16(rows * len(pieces), width),
        in_specs=[VMEM] * len(pieces),
        out_specs=VMEM,
    )(*pieces)


def terms_kernel(scalars, rows_id, cols_id, before, t0, t1, i0, i1, i2, i3, *refs):
    *far, scaled, sums, text, image = refs
    temp = scalars[0]
    offset = scalars[1]
    for n, src in enumerate((t0, t1)):
        text[192 * n : 192 * (n + 1), :] = src[...]
    for n, src in enumerate((i0, i1, i2, i3)):
        image[192 * n : 192 * (n + 1), :] = src[...]
    totals = [before[n] for n in range(3)]
    cols = cols_id[...]
    for tile in range(2):
        at = slice(192 * tile, 192 * (tile + 1))
        cosine = lax.dot_general(
            text[at, :], image[...], (((1,), (1,)), ((), ())), preferred_element_type=jnp.float32
        )
        logits = temp * cosine + offset
        same = rows_id[at, :] == cols
        margin = jnp.where(same, -logits, logits)
        decay = jnp.exp(-jnp.abs(margin))
        inverse = 1.0 / (1.0 + decay)
        sigmoid = jnp.where(margin >= 0, inverse, decay * inverse)
        grad = jnp.where(same, -sigmoid, sigmoid)
        loss = jnp.maximum(margin, 0.0) + jnp.log1p(decay)
        scaled[at, :] = grad.astype(jnp.bfloat16)
        for n, value in enumerate((loss, grad, grad * cosine)):
            totals[n] = totals[n] + jnp.sum(value.reshape(24, 8, 768), axis=0)
    if not far:
        for n in range(3):
            sums[n] = totals[n]
        return
    lane = lax.broadcasted_iota(jnp.int32, (8, 128), 1)
    out = jnp.zeros((8, 128), jnp.float32)
    for n in range(3):
        out = jnp.where(lane == n, jnp.sum(totals[n]), out)
    sums[...] = out
    part = lax.dot_general(
        scaled[...], text[...], (((0,), (0,)), ((), ())), preferred_element_type=jnp.float32
    )
    for n, dst in enumerate(far):
        dst[...] = part[192 * n : 192 * (n + 1)].astype(dst.dtype)


def text_kernel(scaled_own, scaled_far, i0, i1, i2, i3, j0, j1, j2, j3, own, next_low, image):
    total = None
    for scaled, parts in ((scaled_own, (i0, i1, i2, i3)), (scaled_far, (j0, j1, j2, j3))):
        for n, src in enumerate(parts):
            image[192 * n : 192 * (n + 1), :] = src[...]
        part = jnp.dot(scaled[...], image[...], preferred_element_type=jnp.float32)
        total = part if total is None else total + part
    own[...] = total[:192]
    next_low[...] = total[192:].astype(next_low.dtype)


def image_kernel(scaled, t0, t1, b0, b1, b2, b3, sums, own, low1, low2, low3, sums_out, text):
    for n, src in enumerate((t0, t1)):
        text[192 * n : 192 * (n + 1), :] = src[...]
    part = lax.dot_general(
        scaled[...], text[...], (((0,), (0,)), ((), ())), preferred_element_type=jnp.float32
    )
    for n, (back, dst) in enumerate(zip((b0, b1, b2, b3), (own, low1, low2, low3))):
        dst[...] = (part[192 * n : 192 * (n + 1)] + back[...].astype(jnp.float32)).astype(dst.dtype)
    sums_out[...] = sums[...]


def add_kernel(own, r1, r2, r3, sums, out_own, low1, low2, low3, sums_out):
    total = own[...] + r1[...].astype(jnp.float32) + r2[...].astype(jnp.float32) + r3[...].astype(jnp.float32)
    out_own[...] = total[:48]
    for n, dst in enumerate((low1, low2, low3), 1):
        dst[...] = total[48 * n : 48 * (n + 1)].astype(dst.dtype)
    sums_out[...] = sums[...]


def near_kernel(own, r1, out_own, low1, low2, low3):
    total = own[...] + r1[...].astype(jnp.float32)
    out_own[...] = total[:48]
    for n, dst in enumerate((low1, low2, low3), 1):
        dst[...] = total[48 * n : 48 * (n + 1)].astype(dst.dtype)


def local(kernel, out_shape, *args, scratch=()):
    return pl.pallas_call(
        kernel,
        out_shape=out_shape,
        in_specs=[SMEM if a.shape == (2,) else VMEM for a in args],
        out_specs=tuple(VMEM for _ in out_shape),
        scratch_shapes=list(scratch),
        compiler_params=pltpu.CompilerParams(vmem_limit_bytes=48 * 1024 * 1024),
    )(*args)


def finish_kernel(scalars, raw, own, r1, r2, r3, out):
    rows = raw[...]
    width = rows.shape[-1]
    grad = own[...] + r1[...].astype(jnp.float32) + r2[...].astype(jnp.float32) + r3[...].astype(jnp.float32)
    grad = grad * scalars[0]
    square = jnp.mean(rows * rows, axis=-1, keepdims=True) + 1e-06
    inner = jnp.sum(rows * grad, axis=-1, keepdims=True)
    out[...] = (grad - rows * (inner / (square * width))) / (jnp.sqrt(square) * math.sqrt(width))


def f32(*shape):
    return jax.ShapeDtypeStruct(shape, jnp.float32)


def b16(*shape):
    return jax.ShapeDtypeStruct(shape, jnp.bfloat16)


def body(image_raw, text_raw, image_ids, text_ids, log_temp, bias):
    pairs, width = image_raw.shape
    total = pairs * 256
    x, y, c = lax.axis_index("x"), lax.axis_index("y"), lax.axis_index("core")
    z = lax.axis_index("zh") * 4 + lax.axis_index("zl")
    image_unit, text_unit = pl.pallas_call(
        unit_kernel,
        out_shape=(b16(pairs, width), b16(pairs, width)),
        in_specs=[VMEM] * 2,
        out_specs=(VMEM, VMEM),
    )(image_raw, text_raw)

    line = join(image_unit, *[send(image_unit, along_first(k), "first") for k in OFFSETS])
    ring = join(text_unit, *[send(text_unit, along_z(k), "zq") for k in ZOFFSETS])
    plane = [line] + [send(line, along_second(k), "second") for k in OFFSETS]
    ring_next = send(ring, pair_up(1), "za")
    plane_far = [send(p, swap, "swap") for p in plane]

    back = (0,) + OFFSETS
    zback = (0,) + ZOFFSETS
    cols_from = []
    for core in (c, 1 - c):
        for k in back:
            for j in back:
                sx = jnp.where(core == 0, x - j, x - k) % 4
                sy = jnp.where(core == 0, y - k, y - j) % 4
                cols_from.append(flat(sx, sy, z, core))
    rows_from = []
    for step in (0, 1):
        start = z + jnp.where(c == 0, -step, step)
        for k in zback:
            rows_from.append(flat(x, y, (start - k) % 8, c))
    cols_id = image_ids.reshape(256, pairs)[jnp.stack(cols_from)].reshape(1, 32 * pairs)
    rows_id = text_ids.reshape(256, pairs)[jnp.stack(rows_from)].reshape(8 * pairs, 1)

    temp = jnp.exp(log_temp[0])
    scalars = jnp.stack([temp, bias[0]])
    text = (ring, ring_next)
    copies = (pltpu.VMEM((384, width), jnp.bfloat16), pltpu.VMEM((768, width), jnp.bfloat16))
    scaled_own, sums = local(
        terms_kernel, (b16(384, 768), f32(3, 8, 768)),
        scalars, rows_id, cols_id[:, :768], jnp.zeros((3, 8, 768), jnp.float32), *text, *plane, scratch=copies,
    )
    *far, scaled_far, sums = local(
        terms_kernel, (b16(192, width),) * 4 + (b16(384, 768), f32(8, 128)),
        scalars, rows_id, cols_id[:, 768:], sums, *text, *plane_far, scratch=copies,
    )
    back = [send(p, swap, "rswap") for p in far]
    text_own, text_next = local(
        text_kernel, (f32(192, width), b16(192, width)), scaled_own, scaled_far, *plane, *plane_far, scratch=copies[1:],
    )
    text_back = send(text_next, pair_up(-1), "rza")
    image_own, *lows, sums = local(
        image_kernel, (f32(192, width),) + (b16(192, width),) * 3 + (f32(8, 128),),
        scaled_own, *text, *back, sums, scratch=copies[:1],
    )
    image_parts = [send(p, along_second(-k), "rsecond") for p, k in zip(lows, OFFSETS)]
    text_own, *lows = local(
        near_kernel, (f32(pairs, width),) + (b16(pairs, width),) * 3, text_own, text_back,
    )
    text_parts = [send(p, along_z(-k), "rzq") for p, k in zip(lows, ZOFFSETS)]

    def spread(sums, axes, count):
        with jax.named_scope("terms"):
            return lax.all_to_all(jnp.broadcast_to(sums[None], (count, 8, 128)), axes, 0, 0, tiled=True).sum(0)

    sums = spread(sums, ("y", "x", "core"), 32)
    image_own, *lows, sums = local(
        add_kernel, (f32(pairs, width),) + (b16(pairs, width),) * 3 + (f32(8, 128),), image_own, *image_parts, sums,
    )
    image_parts = [send(p, along_first(-k), "rfirst") for p, k in zip(lows, OFFSETS)]
    sums = spread(sums, ("zh", "zl"), 8)

    finish = pl.pallas_call(
        finish_kernel,
        out_shape=f32(pairs, width),
        in_specs=[SMEM] + [VMEM] * 5,
        out_specs=VMEM,
    )
    image_grad = finish(scalars, image_raw, image_own, *image_parts)
    text_grad = finish(scalars, text_raw, text_own, *text_parts)
    return (sums[0, 0:1] / total, image_grad, text_grad, sums[0, 2:3] * temp / total, sums[0, 1:2] / total)


def solution(mesh):
    fine = Mesh(mesh.devices.reshape(SIZES), AXES)
    rows = P(AXES, None)
    return jax.shard_map(
        body,
        mesh=fine,
        in_specs=(rows, rows, P(), P(), P(), P()),
        out_specs=(P(), rows, rows, P(), P()),
        check_vma=False,
    )
```

```python
import math

import jax
import jax.numpy as jnp
import numpy as np
from jax import lax
from jax.experimental import pallas as pl
from jax.experimental.pallas import tpu as pltpu
from jax.sharding import Mesh
from jax.sharding import PartitionSpec as P

SIZES = (4, 2, 4, 2, 4)
AXES = ("y", "zh", "x", "core", "zl")
ROWS = 48
OFFSETS = (1, 3, 2)
ANY = pl.BlockSpec(memory_space=pl.ANY)
VMEM = pl.BlockSpec(memory_space=pltpu.VMEM)
SMEM = pl.BlockSpec(memory_space=pltpu.SMEM)


def flat(x, y, z, c):
    return (((y * 2 + z // 4) * 4 + x) * 2 + c) * 4 + z % 4


def send(value, where, name="move"):
    pairs = []
    for y, zh, x, c, zl in np.ndindex(*SIZES):
        z = zh * 4 + zl
        tx, ty, tz, tc = where(x, y, z, c)
        pairs.append((flat(x, y, z, c), flat(tx % 4, ty % 4, tz % 8, tc % 2)))
    with jax.named_scope(name):
        return lax.ppermute(value, AXES, pairs)


def along_first(k):
    return lambda x, y, z, c: (x + k, y, z, c) if c == 0 else (x, y + k, z, c)


def along_second(k):
    return lambda x, y, z, c: (x, y + k, z, c) if c == 0 else (x + k, y, z, c)


def along_z(k):
    return lambda x, y, z, c: (x, y, z + k, c)


def apart(k):
    return lambda x, y, z, c: (x, y, z + k, c) if c == 0 else (x, y, z - k, c)


def across():
    groups = {}
    for y, zh, x, c, zl in np.ndindex(*SIZES):
        groups.setdefault((c, y if c else x), []).append(flat(x, y, zh * 4 + zl, c))
    return list(groups.values())


def swap(x, y, z, c):
    return (x, y, z, 1 - c)


def unit_kernel(image_ref, text_ref, image_out, text_out):
    for src, dst in ((image_ref, image_out), (text_ref, text_out)):
        rows = src[...]
        scale = jnp.sqrt(jnp.mean(rows * rows, axis=-1, keepdims=True) + 1e-06)
        dst[...] = (rows / (scale * math.sqrt(rows.shape[-1]))).astype(jnp.bfloat16)


def stack(out, sources):
    row = 0
    for src in sources:
        out[row : row + src.shape[0], :] = src[...]
        row += src.shape[0]


def line_kernel(i0, i1, i2, i3, t0, t1, line, pair):
    stack(line, (i0, i1, i2, i3))
    stack(pair, (t0, t1))


def ring_kernel(pair, pair_2, own, opposite, message, kept):
    stack(message, (pair, pair_2))
    stack(kept, (own, opposite, pair_2))


def terms_kernel(scalars, rows_id, cols_id, before, *refs):
    pieces, (*far, scaled, sums, text, image) = refs[:6], refs[6:]
    temp = scalars[0]
    offset = scalars[1]
    stack(text, pieces[:2])
    stack(image, pieces[2:])
    totals = [before[n] for n in range(3)]
    cols = cols_id[...]
    for tile in range(2):
        at = slice(192 * tile, 192 * (tile + 1))
        cosine = lax.dot_general(
            text[at, :], image[...], (((1,), (1,)), ((), ())), preferred_element_type=jnp.float32
        )
        logits = temp * cosine + offset
        same = rows_id[at, :] == cols
        margin = jnp.where(same, -logits, logits)
        decay = jnp.exp(-jnp.abs(margin))
        inverse = 1.0 / (1.0 + decay)
        sigmoid = jnp.where(margin >= 0, inverse, decay * inverse)
        grad = jnp.where(same, -sigmoid, sigmoid)
        loss = jnp.maximum(margin, 0.0) + jnp.log1p(decay)
        scaled[at, :] = grad.astype(jnp.bfloat16)
        for n, value in enumerate((loss, grad, grad * cosine)):
            totals[n] = totals[n] + jnp.sum(value.reshape(24, 8, 768), axis=0)
    if not far:
        for n in range(3):
            sums[n] = totals[n]
        return
    lane = lax.broadcasted_iota(jnp.int32, (8, 128), 1)
    out = jnp.zeros((8, 128), jnp.float32)
    for n in range(3):
        out = jnp.where(lane == n, jnp.sum(totals[n]), out)
    sums[...] = out
    far[0][...] = lax.dot_general(
        scaled[...], text[...], (((0,), (0,)), ((), ())), preferred_element_type=jnp.float32
    ).astype(jnp.bfloat16)


def text_kernel(scaled_own, scaled_far, *refs):
    pieces, (own, opposite, pair, last, image) = refs[:8], refs[8:]
    stack(image, pieces[:4])
    total = jnp.dot(scaled_own[...], image[...], preferred_element_type=jnp.float32)
    stack(image, pieces[4:])
    total = total + jnp.dot(scaled_far[...], image[...], preferred_element_type=jnp.float32)
    row = 0
    for dst in (own, opposite, pair, last):
        dst[...] = total[row : row + dst.shape[0]].astype(dst.dtype)
        row += dst.shape[0]


def image_kernel(scaled, sums, more, t0, t1, back, own, low1, low2, low3, sums_out, text):
    stack(text, (t0, t1))
    part = lax.dot_general(
        scaled[...], text[...], (((0,), (0,)), ((), ())), preferred_element_type=jnp.float32
    )
    for n, dst in enumerate((own, low1, low2, low3)):
        at = slice(192 * n, 192 * (n + 1))
        dst[...] = (part[at] + back[at].astype(jnp.float32)).astype(dst.dtype)
    sums_out[...] = jnp.broadcast_to((sums[...] + more[...])[None], sums_out.shape)


def near_kernel(own, pair, back, opposite, out_own, out_far, low):
    out_own[...] = own[...] + back[:48].astype(jnp.float32) + opposite[...].astype(jnp.float32)
    out_far[...] = back[48:96].astype(jnp.float32)
    low[...] = (pair[...] + back[96:].astype(jnp.float32)).astype(low.dtype)


def add_kernel(own, r1, r2, r3, terms, out_own, low1, low2, low3, sums):
    total = own[...] + r1[...].astype(jnp.float32) + r2[...].astype(jnp.float32) + r3[...].astype(jnp.float32)
    out_own[...] = total[:48]
    value = jnp.sum(terms[...], axis=0)
    sums[...] = value
    high = value[0:1].astype(jnp.bfloat16)
    rest = value[0:1] - high.astype(jnp.float32)
    mid = rest.astype(jnp.bfloat16)
    low = (rest - mid.astype(jnp.float32)).astype(jnp.bfloat16)
    row = lax.broadcasted_iota(jnp.int32, (16, 128), 0)
    parts = [jnp.broadcast_to(v.astype(jnp.float32), (16, 128)) for v in (high, mid, low)]
    extra = jnp.where(row == 0, parts[0], jnp.where(row == 1, parts[1], jnp.where(row == 2, parts[2], 0.0)))
    for n, dst in enumerate((low1, low2, low3), 1):
        dst[:48, :] = total[48 * n : 48 * (n + 1)].astype(dst.dtype)
        dst[48:, :] = jnp.zeros((16, dst.shape[1]), dst.dtype)
        dst[48:, :128] = extra.astype(dst.dtype)


def far_kernel(own, far, back, after, out_own, low):
    out_own[...] = own[...] + back[:48].astype(jnp.float32)
    low[...] = (far[...] + back[48:].astype(jnp.float32)).astype(low.dtype)


def finish_kernel(scalars, image_raw, image_own, i1, i2, i3, text_raw, text_own, t1, sums, image_out, text_out, sums_out):
    for raw, own, parts, out in (
        (image_raw, image_own, (i1, i2, i3), image_out), (text_raw, text_own, (t1,), text_out),
    ):
        rows = raw[...]
        width = rows.shape[-1]
        grad = own[...]
        for part in parts:
            grad = grad + part[:48].astype(jnp.float32)
        grad = grad * scalars[0]
        square = jnp.mean(rows * rows, axis=-1, keepdims=True) + 1e-06
        inner = jnp.sum(rows * grad, axis=-1, keepdims=True)
        out[...] = (grad - rows * (inner / (square * width))) / (jnp.sqrt(square) * math.sqrt(width))
    values = [sums[0:1]]
    for part in (i1, i2, i3):
        extra = part[48:64, :128].astype(jnp.float32)
        values.append((extra[2:3] + extra[1:2]) + extra[0:1])
    sums_out[...] = jnp.broadcast_to((values[0] + values[3]) + (values[1] + values[2]), sums_out.shape)


def f32(*shape):
    return jax.ShapeDtypeStruct(shape, jnp.float32)


def b16(*shape):
    return jax.ShapeDtypeStruct(shape, jnp.bfloat16)


def local(kernel, out_shape, *args, after=(), scratch=()):
    return pl.pallas_call(
        kernel,
        out_shape=out_shape,
        in_specs=[SMEM if a.shape == (2,) else VMEM for a in args] + [ANY] * len(after),
        out_specs=tuple(VMEM for _ in out_shape),
        scratch_shapes=list(scratch),
        compiler_params=pltpu.CompilerParams(vmem_limit_bytes=48 * 1024 * 1024),
    )(*args, *after)


def body(image_raw, text_raw, image_ids, text_ids, log_temp, bias):
    pairs, width = image_raw.shape
    total = pairs * 256
    x, y, c = lax.axis_index("x"), lax.axis_index("y"), lax.axis_index("core")
    z = lax.axis_index("zh") * 4 + lax.axis_index("zl")
    image_unit, text_unit = pl.pallas_call(
        unit_kernel,
        out_shape=(b16(pairs, width), b16(pairs, width)),
        in_specs=[VMEM] * 2,
        out_specs=(VMEM, VMEM),
    )(image_raw, text_raw)

    parts = [send(image_unit, along_first(k), "first") for k in OFFSETS]
    other = send(text_unit, swap, "pair")
    opposite = send(text_unit, along_z(4), "z4")
    line, pair = local(
        line_kernel, (b16(4 * pairs, width), b16(2 * pairs, width)), image_unit, *parts, text_unit, other,
    )
    plane = [line] + [send(line, along_second(k), "second") for k in OFFSETS]
    message, kept = local(
        ring_kernel, (b16(4 * pairs, width),) * 2, pair, send(pair, apart(2), "z2"), text_unit, opposite,
    )
    text = (kept, send(message, apart(1), "z1"))
    plane_far = [send(p, swap, "swap") for p in plane]

    back = (0,) + OFFSETS
    cols_from = []
    for core in (c, 1 - c):
        for k in back:
            for j in back:
                sx = jnp.where(core == 0, x - j, x - k) % 4
                sy = jnp.where(core == 0, y - k, y - j) % 4
                cols_from.append(flat(sx, sy, z, core))
    step = jnp.where(c == 0, 1, -1)
    rows_from = [flat(x, y, z, c), flat(x, y, (z + 4) % 8, c)]
    for k in (2, 1, 3):
        rows_from += [flat(x, y, (z - k * step) % 8, core) for core in (c, 1 - c)]
    cols_id = image_ids.reshape(256, pairs)[jnp.stack(cols_from)].reshape(1, 32 * pairs)
    rows_id = text_ids.reshape(256, pairs)[jnp.stack(rows_from)].reshape(8 * pairs, 1)

    temp = jnp.exp(log_temp[0])
    scalars = jnp.stack([temp, bias[0]])
    copies = (pltpu.VMEM((384, width), jnp.bfloat16), pltpu.VMEM((768, width), jnp.bfloat16))
    scaled_own, sums = local(
        terms_kernel, (b16(384, 768), f32(3, 8, 768)),
        scalars, rows_id, cols_id[:, :768], jnp.zeros((3, 8, 768), jnp.float32), *text, *plane, scratch=copies,
    )
    far, scaled_far, sums = local(
        terms_kernel, (b16(768, width), b16(384, 768), f32(8, 128)),
        scalars, rows_id, cols_id[:, 768:], sums, *text, *plane_far, scratch=copies,
    )
    back = send(far, swap, "rswap")
    sums_core = send(sums, swap, "sums")
    text_own, opposite_low, text_pair, last = local(
        text_kernel, (f32(pairs, width), b16(pairs, width), f32(2 * pairs, width), b16(4 * pairs, width)),
        scaled_own, scaled_far, *plane, *plane_far, scratch=copies[1:],
    )
    last = send(last, apart(-1), "rz1")
    opposite_back = send(opposite_low, along_z(4), "rz4")
    image_own, *lows, spread = local(
        image_kernel, (f32(192, width),) + (b16(192, width),) * 3 + (f32(32, 8, 128),),
        scaled_own, sums, sums_core, *text, back, scratch=copies[:1],
    )
    image_parts = [send(p, along_second(-k), "rsecond") for p, k in zip(lows, OFFSETS)]
    text_own, text_far, low = local(
        near_kernel, (f32(pairs, width), f32(pairs, width), b16(2 * pairs, width)),
        text_own, text_pair, last, opposite_back,
    )
    back = send(low, apart(-2), "rz2")
    with jax.named_scope("terms"):
        spread = lax.all_to_all(spread, AXES, 0, 0, tiled=True, axis_index_groups=across())
    image_own, *lows, sums = local(
        add_kernel, (f32(pairs, width),) + (b16(pairs + 16, width),) * 3 + (f32(8, 128),),
        image_own, *image_parts, spread,
    )
    image_parts = [send(p, along_first(-k), "rfirst") for p, k in zip(lows, OFFSETS)]
    text_own, far_low = local(
        far_kernel, (f32(pairs, width), b16(pairs, width)), text_own, text_far, back, after=(image_own,),
    )
    image_grad, text_grad, sums = local(
        finish_kernel, (f32(pairs, width),) * 2 + (f32(8, 128),),
        scalars, image_raw, image_own, *image_parts, text_raw, text_own, send(far_low, swap, "rpair"), sums,
    )
    return (sums[0, 0:1] / total, image_grad, text_grad, sums[0, 2:3] * temp / total, sums[0, 1:2] / total)


def solution(mesh):
    fine = Mesh(mesh.devices.reshape(SIZES), AXES)
    rows = P(AXES, None)
    return jax.shard_map(
        body,
        mesh=fine,
        in_specs=(rows, rows, P(), P(), P(), P()),
        out_specs=(P(), rows, rows, P(), P()),
        check_vma=False,
    )
```

```python
import math

import jax
import jax.numpy as jnp
import numpy as np
from jax import lax
from jax.experimental import pallas as pl
from jax.experimental.pallas import tpu as pltpu
from jax.sharding import Mesh
from jax.sharding import PartitionSpec as P

SIZES = (4, 2, 4, 2, 4)
AXES = ("y", "zh", "x", "core", "zl")
ROWS = 48
OFFSETS = (1, 3, 2)
ANY = pl.BlockSpec(memory_space=pl.ANY)
VMEM = pl.BlockSpec(memory_space=pltpu.VMEM)
SMEM = pl.BlockSpec(memory_space=pltpu.SMEM)


def flat(x, y, z, c):
    return (((y * 2 + z // 4) * 4 + x) * 2 + c) * 4 + z % 4


def send(value, where, name="move"):
    pairs = []
    for y, zh, x, c, zl in np.ndindex(*SIZES):
        z = zh * 4 + zl
        tx, ty, tz, tc = where(x, y, z, c)
        pairs.append((flat(x, y, z, c), flat(tx % 4, ty % 4, tz % 8, tc % 2)))
    with jax.named_scope(name):
        return lax.ppermute(value, AXES, pairs)


def along_first(k):
    return lambda x, y, z, c: (x + k, y, z, c) if c == 0 else (x, y + k, z, c)


def along_second(k):
    return lambda x, y, z, c: (x, y + k, z, c) if c == 0 else (x + k, y, z, c)


def along_z(k):
    return lambda x, y, z, c: (x, y, z + k, c)


def apart(k):
    return lambda x, y, z, c: (x, y, z + k, c) if c == 0 else (x, y, z - k, c)


def across():
    groups = {}
    for y, zh, x, c, zl in np.ndindex(*SIZES):
        groups.setdefault((c, y if c else x), []).append(flat(x, y, zh * 4 + zl, c))
    return list(groups.values())


def swap(x, y, z, c):
    return (x, y, z, 1 - c)


def unit(rows):
    scale = jnp.sqrt(jnp.mean(rows * rows, axis=-1, keepdims=True) + 1e-06)
    return (rows / (scale * math.sqrt(rows.shape[-1]))).astype(jnp.bfloat16)


def text_unit_kernel(raw, out, kept):
    out[...] = unit(raw[...])
    kept[...] = out[...]


def image_unit_kernel(raw, text, text_far, out, kept, pair, pair_kept):
    out[...] = unit(raw[...])
    kept[...] = out[...]
    stack(pair, (text, text_far))
    stack(pair_kept, (text, text_far))


def stack(out, sources):
    row = 0
    for src in sources:
        out[row : row + src.shape[0], :] = src[...]
        row += src.shape[0]


def gather_kernel(i0, i1, i2, i3, own, pair, pair_2, after, line, message, hop, kept):
    stack(line, (i0, i1, i2, i3))
    stack(message, (pair, pair_2))
    hop[...] = pair_2[:48]
    stack(kept, (own, pair_2))


def flag_kernel(*refs):
    refs[-1][...] = jnp.zeros_like(refs[-1])


def copy_kernel(src, after, out):
    out[...] = src[...]


def ride(out, row, value):
    high = value.astype(jnp.bfloat16).astype(jnp.float32)
    mid = (value - high).astype(jnp.bfloat16).astype(jnp.float32)
    low = value - high - mid
    at = lax.broadcasted_iota(jnp.int32, (16, 128), 0)
    extra = jnp.where(at == 0, high, jnp.where(at == 1, mid, jnp.where(at == 2, low, 0.0)))
    out[row:, :] = jnp.zeros((16, out.shape[1]), out.dtype)
    out[row:, :128] = extra.astype(out.dtype)


def alight(part, row):
    extra = part[row : row + 16, :128].astype(jnp.float32)
    return (extra[2:3] + extra[1:2]) + extra[0:1]


def terms_kernel(scalars, rows_id, cols_id, before, *refs):
    pieces, (*far, scaled, sums, text, image) = refs[:7], refs[7:]
    temp = scalars[0]
    offset = scalars[1]
    stack(text, pieces[:3])
    stack(image, pieces[3:])
    totals = [before[n] for n in range(3)]
    cols = cols_id[...]
    rows = jnp.transpose(jnp.broadcast_to(rows_id[...].astype(jnp.float32), (128, 384)))[:, :1].astype(jnp.int32)
    for tile in range(2):
        at = slice(192 * tile, 192 * (tile + 1))
        cosine = lax.dot_general(
            text[at, :], image[...], (((1,), (1,)), ((), ())), preferred_element_type=jnp.float32
        )
        logits = temp * cosine + offset
        same = rows[at, :] == cols
        margin = jnp.where(same, -logits, logits)
        decay = jnp.exp(-jnp.abs(margin))
        inverse = 1.0 / (1.0 + decay)
        sigmoid = jnp.where(margin >= 0, inverse, decay * inverse)
        grad = jnp.where(same, -sigmoid, sigmoid)
        loss = jnp.maximum(margin, 0.0) + jnp.log1p(decay)
        scaled[at, :] = grad.astype(jnp.bfloat16)
        for n, value in enumerate((loss, grad, grad * cosine)):
            totals[n] = totals[n] + jnp.sum(value.reshape(24, 8, 768), axis=0)
    if not far:
        for n in range(3):
            sums[n] = totals[n]
        return
    lane = lax.broadcasted_iota(jnp.int32, (1, 128), 1)
    out = jnp.zeros((1, 128), jnp.float32)
    for n in range(3):
        out = jnp.where(lane == n, jnp.sum(totals[n]), out)
    sums[...] = jnp.broadcast_to(out, sums.shape)
    far[0][:768, :] = lax.dot_general(
        scaled[...], text[...], (((0,), (0,)), ((), ())), preferred_element_type=jnp.float32
    ).astype(jnp.bfloat16)
    ride(far[0], 768, out)


def text_kernel(scaled_own, scaled_far, *refs):
    pieces, (own, pair, opposite, last, image) = refs[:8], refs[8:]
    stack(image, pieces[:4])
    total = jnp.dot(scaled_own[...], image[...], preferred_element_type=jnp.float32)
    stack(image, pieces[4:])
    total = total + jnp.dot(scaled_far[...], image[...], preferred_element_type=jnp.float32)
    row = 0
    for dst in (own, pair, opposite, last):
        dst[...] = total[row : row + dst.shape[0]].astype(dst.dtype)
        row += dst.shape[0]


def image_kernel(scaled, sums, t0, t1, t2, back, own, low1, low2, low3, sums_out, text):
    stack(text, (t0, t1, t2))
    part = lax.dot_general(
        scaled[...], text[...], (((0,), (0,)), ((), ())), preferred_element_type=jnp.float32
    )
    for n, dst in enumerate((own, low1, low2, low3)):
        at = slice(192 * n, 192 * (n + 1))
        dst[...] = (part[at] + back[at].astype(jnp.float32)).astype(dst.dtype)
    sums_out[...] = jnp.broadcast_to((sums[...] + alight(back, 768))[None], sums_out.shape)


def near_kernel(own, pair, back, hop, out_own, out_far, low):
    out_own[...] = own[...] + back[:48].astype(jnp.float32)
    out_far[...] = back[48:96].astype(jnp.float32)
    total = pair[...] + back[96:].astype(jnp.float32)
    low[:48] = (total[:48] + hop[...].astype(jnp.float32)).astype(low.dtype)
    low[48:] = total[48:].astype(low.dtype)


def add_kernel(own, r1, r2, r3, terms, out_own, low1, low2, low3, sums):
    total = own[...] + r1[...].astype(jnp.float32) + r2[...].astype(jnp.float32) + r3[...].astype(jnp.float32)
    out_own[...] = total[:48]
    value = jnp.sum(terms[...], axis=0)
    sums[...] = value
    for n, dst in enumerate((low1, low2, low3), 1):
        dst[:48, :] = total[48 * n : 48 * (n + 1)].astype(dst.dtype)
        ride(dst, 48, value[:1])


def far_kernel(own, far, back, after, out_own, low):
    out_own[...] = own[...] + back[:48].astype(jnp.float32)
    low[...] = (far[...] + back[48:].astype(jnp.float32)).astype(low.dtype)


def finish_kernel(scalars, image_raw, image_own, i1, i2, i3, text_raw, text_own, t1, sums,
                  image_out, text_out, loss, bias_grad, temp_grad):
    for raw, own, parts, out in (
        (image_raw, image_own, (i1, i2, i3), image_out), (text_raw, text_own, (t1,), text_out),
    ):
        rows = raw[...]
        width = rows.shape[-1]
        grad = own[...]
        for part in parts:
            grad = grad + part[:48].astype(jnp.float32)
        grad = grad * scalars[0]
        square = jnp.mean(rows * rows, axis=-1, keepdims=True) + 1e-06
        inner = jnp.sum(rows * grad, axis=-1, keepdims=True)
        out[...] = (grad - rows * (inner / (square * width))) / (jnp.sqrt(square) * math.sqrt(width))
    values = [sums[0:1]] + [alight(part, 48) for part in (i1, i2, i3)]
    total = (values[0] + values[3]) + (values[1] + values[2])
    lane = lax.broadcasted_iota(jnp.int32, total.shape, 1)
    for n, (out, factor) in enumerate(((loss, 1.0), (bias_grad, 1.0), (temp_grad, scalars[0]))):
        out[0] = jnp.sum(jnp.where(lane == n, total, 0.0)) * factor / (48 * 256)


def f32(*shape):
    return jax.ShapeDtypeStruct(shape, jnp.float32)


def b16(*shape):
    return jax.ShapeDtypeStruct(shape, jnp.bfloat16)


def local(kernel, out_shape, *args, after=(), scratch=(), grant=8):
    return pl.pallas_call(
        kernel,
        out_shape=out_shape,
        in_specs=[SMEM if a.shape == (2,) else VMEM for a in args] + [ANY] * len(after),
        out_specs=tuple(SMEM if o.shape == (1,) else VMEM for o in out_shape),
        scratch_shapes=list(scratch),
        compiler_params=pltpu.CompilerParams(vmem_limit_bytes=grant * 1024 * 1024),
    )(*args, *after)


def body(image_raw, text_raw, image_ids, text_ids, log_temp, bias):
    pairs, width = image_raw.shape
    x, y, c = lax.axis_index("x"), lax.axis_index("y"), lax.axis_index("core")
    z = lax.axis_index("zh") * 4 + lax.axis_index("zl")
    text_unit, text_kept = local(text_unit_kernel, (b16(pairs, width),) * 2, text_raw)
    image_unit, image_kept, pair, pair_kept = local(
        image_unit_kernel, (b16(pairs, width),) * 2 + (b16(2 * pairs, width),) * 2,
        image_raw, text_kept, send(text_unit, swap, "pair"),
    )

    parts = [send(image_unit, along_first(k), "first") for k in OFFSETS]
    pair_2 = send(pair, apart(2), "z2")
    (flag,) = local(flag_kernel, (f32(8, 128),), after=parts)
    flag = send(flag, swap, "flag")
    line, message, hop, kept = local(
        gather_kernel, (b16(4 * pairs, width),) * 2 + (b16(pairs, width), b16(3 * pairs, width)),
        image_kept, *parts, text_kept, pair_kept, pair_2, after=(flag,),
    )

    plane = [line] + [send(line, along_second(k), "second") for k in OFFSETS]
    text = (kept, send(hop, apart(2), "z4"), send(message, apart(1), "z1"))
    (line_kept,) = local(copy_kernel, (b16(4 * pairs, width),), line, after=(plane[1],))
    plane_far = [send(p, swap, "swap") for p in [line_kept] + plane[1:]]

    back = (0,) + OFFSETS
    cols_from = []
    for core in (c, 1 - c):
        for k in back:
            for j in back:
                sx = jnp.where(core == 0, x - j, x - k) % 4
                sy = jnp.where(core == 0, y - k, y - j) % 4
                cols_from.append(flat(sx, sy, z, core))
    step = jnp.where(c == 0, 1, -1)
    rows_from = [flat(x, y, z, c)]
    for k in (2, 4, 1, 3):
        rows_from += [flat(x, y, (z - k * step) % 8, core) for core in ((c,) if k == 4 else (c, 1 - c))]
    cols_id = image_ids.reshape(256, pairs)[jnp.stack(cols_from)].reshape(1, 32 * pairs)
    rows_id = text_ids.reshape(256, pairs)[jnp.stack(rows_from)].reshape(1, 8 * pairs)

    temp = jnp.exp(log_temp[0])
    scalars = jnp.stack([temp, bias[0]])
    copies = (pltpu.VMEM((384, width), jnp.bfloat16), pltpu.VMEM((768, width), jnp.bfloat16))
    scaled_own, sums = local(
        terms_kernel, (b16(384, 768), f32(3, 8, 768)),
        scalars, rows_id, cols_id[:, :768], jnp.zeros((3, 8, 768), jnp.float32), *text, *plane, scratch=copies, grant=16,
    )
    far, scaled_far, sums = local(
        terms_kernel, (b16(784, width), b16(384, 768), f32(8, 128)),
        scalars, rows_id, cols_id[:, 768:], sums, *text, *plane_far, scratch=copies, grant=16,
    )
    back = send(far, swap, "rswap")
    text_own, text_pair, hop, last = local(
        text_kernel, (f32(pairs, width), f32(2 * pairs, width), b16(pairs, width), b16(4 * pairs, width)),
        scaled_own, scaled_far, *plane, *plane_far, scratch=copies[1:], grant=16,
    )
    last = send(last, apart(-1), "rz1")
    hop = send(hop, apart(-2), "rz4")
    image_own, *lows, spread = local(
        image_kernel, (f32(192, width),) + (b16(192, width),) * 3 + (f32(32, 8, 128),),
        scaled_own, sums, *text, back, scratch=copies[:1], grant=16,
    )
    image_parts = [send(p, along_second(-k), "rsecond") for p, k in zip(lows, OFFSETS)]
    text_own, text_far, low = local(
        near_kernel, (f32(pairs, width), f32(pairs, width), b16(2 * pairs, width)),
        text_own, text_pair, last, hop,
    )
    back = send(low, apart(-2), "rz2")
    with jax.named_scope("terms"):
        spread = lax.all_to_all(spread, AXES, 0, 0, tiled=True, axis_index_groups=across())
    image_own, *lows, sums = local(
        add_kernel, (f32(pairs, width),) + (b16(pairs + 16, width),) * 3 + (f32(8, 128),),
        image_own, *image_parts, spread,
    )
    image_parts = [send(p, along_first(-k), "rfirst") for p, k in zip(lows, OFFSETS)]
    text_own, far_low = local(
        far_kernel, (f32(pairs, width), b16(pairs, width)), text_own, text_far, back, after=(image_own,),
    )
    image_grad, text_grad, loss, bias_grad, temp_grad = local(
        finish_kernel, (f32(pairs, width),) * 2 + (f32(1),) * 3,
        scalars, image_raw, image_own, *image_parts, text_raw, text_own, send(far_low, swap, "rpair"), sums,
    )
    return (loss, image_grad, text_grad, temp_grad, bias_grad)


def solution(mesh):
    fine = Mesh(mesh.devices.reshape(SIZES), AXES)
    rows = P(AXES, None)
    return jax.shard_map(
        body,
        mesh=fine,
        in_specs=(rows, rows, P(), P(), P(), P()),
        out_specs=(P(), rows, rows, P(), P()),
        check_vma=False,
    )
```

```python
import math

import jax
import jax.numpy as jnp
import numpy as np
from jax import lax
from jax.experimental import pallas as pl
from jax.experimental.pallas import tpu as pltpu
from jax.sharding import Mesh
from jax.sharding import PartitionSpec as P

SIZES = (4, 2, 4, 2, 4)
AXES = ("y", "zh", "x", "core", "zl")
ROWS = 48
OFFSETS = (1, 3, 2)
ANY = pl.BlockSpec(memory_space=pl.ANY)
VMEM = pl.BlockSpec(memory_space=pltpu.VMEM)
SMEM = pl.BlockSpec(memory_space=pltpu.SMEM)


def flat(x, y, z, c):
    return (((y * 2 + z // 4) * 4 + x) * 2 + c) * 4 + z % 4


def send(value, where, name="move"):
    pairs = []
    for y, zh, x, c, zl in np.ndindex(*SIZES):
        z = zh * 4 + zl
        tx, ty, tz, tc = where(x, y, z, c)
        pairs.append((flat(x, y, z, c), flat(tx % 4, ty % 4, tz % 8, tc % 2)))
    with jax.named_scope(name):
        return lax.ppermute(value, AXES, pairs)


def along_first(k):
    return lambda x, y, z, c: (x + k, y, z, c) if c == 0 else (x, y + k, z, c)


def along_second(k):
    return lambda x, y, z, c: (x, y + k, z, c) if c == 0 else (x + k, y, z, c)


def along_z(k):
    return lambda x, y, z, c: (x, y, z + k, c)


def apart(k):
    return lambda x, y, z, c: (x, y, z + k, c) if c == 0 else (x, y, z - k, c)


def across():
    groups = {}
    for y, zh, x, c, zl in np.ndindex(*SIZES):
        groups.setdefault((c, y if c else x), []).append(flat(x, y, zh * 4 + zl, c))
    return list(groups.values())


def swap(x, y, z, c):
    return (x, y, z, 1 - c)


def unit(rows):
    scale = jnp.sqrt(jnp.mean(rows * rows, axis=-1, keepdims=True) + 1e-06)
    return (rows / (scale * math.sqrt(rows.shape[-1]))).astype(jnp.bfloat16)


def text_unit_kernel(raw, out, kept):
    out[...] = unit(raw[...])
    kept[...] = out[...]


def image_unit_kernel(raw, after, far_after, out, kept):
    out[...] = unit(raw[...])
    kept[...] = out[...]


def pair_kernel(text, text_far, after, pair, kept):
    stack(pair, (text, text_far))
    stack(kept, (text, text_far))


def stack(out, sources):
    row = 0
    for src in sources:
        out[row : row + src.shape[0], :] = src[...]
        row += src.shape[0]


def gather_kernel(i0, i1, i2, i3, own, pair, pair_2, after, cols_after, rows_after, line, message, hop, kept):
    stack(line, (i0, i1, i2, i3))
    stack(message, (pair, pair_2))
    hop[...] = pair_2[:48]
    stack(kept, (own, pair_2))


def flag_kernel(*refs):
    refs[-1][...] = jnp.zeros_like(refs[-1])


def copy_kernel(src, after, out):
    out[...] = src[...]


def ride(out, row, value):
    high = value.astype(jnp.bfloat16).astype(jnp.float32)
    mid = (value - high).astype(jnp.bfloat16).astype(jnp.float32)
    low = value - high - mid
    at = lax.broadcasted_iota(jnp.int32, (16, 128), 0)
    extra = jnp.where(at == 0, high, jnp.where(at == 1, mid, jnp.where(at == 2, low, 0.0)))
    out[row:, :] = jnp.zeros((16, out.shape[1]), out.dtype)
    out[row:, :128] = extra.astype(out.dtype)


def alight(part, row):
    extra = part[row : row + 16, :128].astype(jnp.float32)
    return (extra[2:3] + extra[1:2]) + extra[0:1]


def terms_kernel(scalars, rows_id, cols_id, before, *refs):
    pieces, (*far, scaled, sums, text, image) = refs[:7], refs[7:]
    temp = scalars[0]
    offset = scalars[1]
    stack(text, pieces[:3])
    stack(image, pieces[3:])
    totals = [before[n] for n in range(3)]
    cols = cols_id[...]
    rows = jnp.transpose(jnp.broadcast_to(rows_id[...].astype(jnp.float32), (128, 384)))[:, :1].astype(jnp.int32)
    for tile in range(2):
        at = slice(192 * tile, 192 * (tile + 1))
        cosine = lax.dot_general(
            text[at, :], image[...], (((1,), (1,)), ((), ())), preferred_element_type=jnp.float32
        )
        logits = temp * cosine + offset
        same = rows[at, :] == cols
        margin = jnp.where(same, -logits, logits)
        decay = jnp.exp(-jnp.abs(margin))
        inverse = 1.0 / (1.0 + decay)
        sigmoid = jnp.where(margin >= 0, inverse, decay * inverse)
        grad = jnp.where(same, -sigmoid, sigmoid)
        loss = jnp.maximum(margin, 0.0) + jnp.log1p(decay)
        scaled[at, :] = grad.astype(jnp.bfloat16)
        for n, value in enumerate((loss, grad, grad * cosine)):
            totals[n] = totals[n] + jnp.sum(value.reshape(24, 8, 768), axis=0)
    if not far:
        for n in range(3):
            sums[n] = totals[n]
        return
    lane = lax.broadcasted_iota(jnp.int32, (1, 128), 1)
    out = jnp.zeros((1, 128), jnp.float32)
    for n in range(3):
        out = jnp.where(lane == n, jnp.sum(totals[n]), out)
    sums[...] = jnp.broadcast_to(out, sums.shape)
    far[0][:768, :] = lax.dot_general(
        scaled[...], text[...], (((0,), (0,)), ((), ())), preferred_element_type=jnp.float32
    ).astype(jnp.bfloat16)
    ride(far[0], 768, out)


def text_kernel(scaled_own, scaled_far, *refs):
    pieces, (own, pair, opposite, last, image) = refs[:8], refs[8:]
    stack(image, pieces[:4])
    total = jnp.dot(scaled_own[...], image[...], preferred_element_type=jnp.float32)
    stack(image, pieces[4:])
    total = total + jnp.dot(scaled_far[...], image[...], preferred_element_type=jnp.float32)
    row = 0
    for dst in (own, pair, opposite, last):
        dst[...] = total[row : row + dst.shape[0]].astype(dst.dtype)
        row += dst.shape[0]


def image_kernel(scaled, sums, t0, t1, t2, back, own, low1, low2, low3, sums_out, text):
    stack(text, (t0, t1, t2))
    part = lax.dot_general(
        scaled[...], text[...], (((0,), (0,)), ((), ())), preferred_element_type=jnp.float32
    )
    for n, dst in enumerate((own, low1, low2, low3)):
        at = slice(192 * n, 192 * (n + 1))
        dst[...] = (part[at] + back[at].astype(jnp.float32)).astype(dst.dtype)
    sums_out[...] = jnp.broadcast_to((sums[...] + alight(back, 768))[None], sums_out.shape)


def near_kernel(own, pair, back, hop, out_own, out_far, low):
    out_own[...] = own[...] + back[:48].astype(jnp.float32)
    out_far[...] = back[48:96].astype(jnp.float32)
    total = pair[...] + back[96:].astype(jnp.float32)
    low[:48] = (total[:48] + hop[...].astype(jnp.float32)).astype(low.dtype)
    low[48:] = total[48:].astype(low.dtype)


def add_kernel(own, r1, r2, r3, terms, out_own, low1, low2, low3, sums):
    total = own[...] + r1[...].astype(jnp.float32) + r2[...].astype(jnp.float32) + r3[...].astype(jnp.float32)
    out_own[...] = total[:48]
    value = jnp.sum(terms[...], axis=0)
    sums[...] = value
    for n, dst in enumerate((low1, low2, low3), 1):
        dst[:48, :] = total[48 * n : 48 * (n + 1)].astype(dst.dtype)
        ride(dst, 48, value[:1])


def far_kernel(own, far, back, after, out_own, low):
    out_own[...] = own[...] + back[:48].astype(jnp.float32)
    low[...] = (far[...] + back[48:].astype(jnp.float32)).astype(low.dtype)


def finish_kernel(scalars, image_raw, image_own, i1, i2, i3, text_raw, text_own, t1, sums,
                  image_out, text_out, loss, bias_grad, temp_grad):
    for raw, own, parts, out in (
        (image_raw, image_own, (i1, i2, i3), image_out), (text_raw, text_own, (t1,), text_out),
    ):
        rows = raw[...]
        width = rows.shape[-1]
        grad = own[...]
        for part in parts:
            grad = grad + part[:48].astype(jnp.float32)
        grad = grad * scalars[0]
        square = jnp.mean(rows * rows, axis=-1, keepdims=True) + 1e-06
        inner = jnp.sum(rows * grad, axis=-1, keepdims=True)
        out[...] = (grad - rows * (inner / (square * width))) / (jnp.sqrt(square) * math.sqrt(width))
    values = [sums[0:1]] + [alight(part, 48) for part in (i1, i2, i3)]
    total = (values[0] + values[3]) + (values[1] + values[2])
    lane = lax.broadcasted_iota(jnp.int32, total.shape, 1)
    for n, (out, factor) in enumerate(((loss, 1.0), (bias_grad, 1.0), (temp_grad, scalars[0]))):
        out[0] = jnp.sum(jnp.where(lane == n, total, 0.0)) * factor / (48 * 256)


def f32(*shape):
    return jax.ShapeDtypeStruct(shape, jnp.float32)


def b16(*shape):
    return jax.ShapeDtypeStruct(shape, jnp.bfloat16)


def local(kernel, out_shape, *args, after=(), scratch=(), grant=8):
    return pl.pallas_call(
        kernel,
        out_shape=out_shape,
        in_specs=[SMEM if a.shape == (2,) else VMEM for a in args] + [ANY] * len(after),
        out_specs=tuple(SMEM if o.shape == (1,) else VMEM for o in out_shape),
        scratch_shapes=list(scratch),
        compiler_params=pltpu.CompilerParams(vmem_limit_bytes=grant * 1024 * 1024),
    )(*args, *after)


def body(image_raw, text_raw, image_ids, text_ids, log_temp, bias):
    pairs, width = image_raw.shape
    x, y, c = lax.axis_index("x"), lax.axis_index("y"), lax.axis_index("core")
    z = lax.axis_index("zh") * 4 + lax.axis_index("zl")
    text_unit, text_kept = local(text_unit_kernel, (b16(pairs, width),) * 2, text_raw)
    text_far = send(text_unit, swap, "pair")
    image_unit, image_kept = local(image_unit_kernel, (b16(pairs, width),) * 2, image_raw, after=(text_kept, text_far))
    pair, pair_kept = local(
        pair_kernel, (b16(2 * pairs, width),) * 2, text_kept, text_far, after=(image_kept,),
    )

    parts = [send(image_unit, along_first(k), "first") for k in OFFSETS]
    pair_2 = send(pair, apart(2), "z2")
    back = (0,) + OFFSETS
    cols_from = []
    for core in (c, 1 - c):
        for k in back:
            for j in back:
                sx = jnp.where(core == 0, x - j, x - k) % 4
                sy = jnp.where(core == 0, y - k, y - j) % 4
                cols_from.append(flat(sx, sy, z, core))
    step = jnp.where(c == 0, 1, -1)
    rows_from = [flat(x, y, z, c)]
    for k in (2, 4, 1, 3):
        rows_from += [flat(x, y, (z - k * step) % 8, core) for core in ((c,) if k == 4 else (c, 1 - c))]
    cols_id = image_ids.reshape(256, pairs)[jnp.stack(cols_from)].reshape(1, 32 * pairs)
    rows_id = text_ids.reshape(256, pairs)[jnp.stack(rows_from)].reshape(1, 8 * pairs)

    (flag,) = local(flag_kernel, (f32(8, 128),), after=parts)
    flag = send(flag, swap, "flag")
    line, message, hop, kept = local(
        gather_kernel, (b16(4 * pairs, width),) * 2 + (b16(pairs, width), b16(3 * pairs, width)),
        image_kept, *parts, text_kept, pair_kept, pair_2, after=(flag, cols_id, rows_id),
    )

    plane = [line] + [send(line, along_second(k), "second") for k in OFFSETS]
    text = (kept, send(hop, apart(2), "z4"), send(message, apart(1), "z1"))
    (line_kept,) = local(copy_kernel, (b16(4 * pairs, width),), line, after=(plane[1],))
    plane_far = [send(p, swap, "swap") for p in [line_kept] + plane[1:]]

    temp = jnp.exp(log_temp[0])
    scalars = jnp.stack([temp, bias[0]])
    copies = (pltpu.VMEM((384, width), jnp.bfloat16), pltpu.VMEM((768, width), jnp.bfloat16))
    scaled_own, sums = local(
        terms_kernel, (b16(384, 768), f32(3, 8, 768)),
        scalars, rows_id, cols_id[:, :768], jnp.zeros((3, 8, 768), jnp.float32), *text, *plane, scratch=copies, grant=16,
    )
    far, scaled_far, sums = local(
        terms_kernel, (b16(784, width), b16(384, 768), f32(8, 128)),
        scalars, rows_id, cols_id[:, 768:], sums, *text, *plane_far, scratch=copies, grant=16,
    )
    back = send(far, swap, "rswap")
    text_own, text_pair, hop, last = local(
        text_kernel, (f32(pairs, width), f32(2 * pairs, width), b16(pairs, width), b16(4 * pairs, width)),
        scaled_own, scaled_far, *plane, *plane_far, scratch=copies[1:], grant=16,
    )
    last = send(last, apart(-1), "rz1")
    hop = send(hop, apart(-2), "rz4")
    image_own, *lows, spread = local(
        image_kernel, (f32(192, width),) + (b16(192, width),) * 3 + (f32(32, 8, 128),),
        scaled_own, sums, *text, back, scratch=copies[:1], grant=16,
    )
    image_parts = [send(p, along_second(-k), "rsecond") for p, k in zip(lows, OFFSETS)]
    text_own, text_far, low = local(
        near_kernel, (f32(pairs, width), f32(pairs, width), b16(2 * pairs, width)),
        text_own, text_pair, last, hop,
    )
    back = send(low, apart(-2), "rz2")
    with jax.named_scope("terms"):
        spread = lax.all_to_all(spread, AXES, 0, 0, tiled=True, axis_index_groups=across())
    image_own, *lows, sums = local(
        add_kernel, (f32(pairs, width),) + (b16(pairs + 16, width),) * 3 + (f32(8, 128),),
        image_own, *image_parts, spread,
    )
    image_parts = [send(p, along_first(-k), "rfirst") for p, k in zip(lows, OFFSETS)]
    text_own, far_low = local(
        far_kernel, (f32(pairs, width), b16(pairs, width)), text_own, text_far, back, after=(image_own,),
    )
    image_grad, text_grad, loss, bias_grad, temp_grad = local(
        finish_kernel, (f32(pairs, width),) * 2 + (f32(1),) * 3,
        scalars, image_raw, image_own, *image_parts, text_raw, text_own, send(far_low, swap, "rpair"), sums,
    )
    return (loss, image_grad, text_grad, temp_grad, bias_grad)


def solution(mesh):
    fine = Mesh(mesh.devices.reshape(SIZES), AXES)
    rows = P(AXES, None)
    return jax.shard_map(
        body,
        mesh=fine,
        in_specs=(rows, rows, P(), P(), P(), P()),
        out_specs=(P(), rows, rows, P(), P()),
        check_vma=False,
    )
```

```python
import functools
import math

import jax
import jax.numpy as jnp
import numpy as np
from jax import lax
from jax.experimental import pallas as pl
from jax.experimental.pallas import tpu as pltpu
from jax.sharding import Mesh
from jax.sharding import PartitionSpec as P

SIZES = (4, 2, 4, 2, 4)
AXES = ("y", "zh", "x", "core", "zl")
ROWS = 48
OFFSETS = (1, 3, 2)
ANY = pl.BlockSpec(memory_space=pl.ANY)
VMEM = pl.BlockSpec(memory_space=pltpu.VMEM)
SMEM = pl.BlockSpec(memory_space=pltpu.SMEM)


def flat(x, y, z, c):
    return (((y * 2 + z // 4) * 4 + x) * 2 + c) * 4 + z % 4


def send(value, where, name="move"):
    pairs = []
    for y, zh, x, c, zl in np.ndindex(*SIZES):
        z = zh * 4 + zl
        tx, ty, tz, tc = where(x, y, z, c)
        pairs.append((flat(x, y, z, c), flat(tx % 4, ty % 4, tz % 8, tc % 2)))
    with jax.named_scope(name):
        return lax.ppermute(value, AXES, pairs)


def along_first(k):
    return lambda x, y, z, c: (x + k, y, z, c) if c == 0 else (x, y + k, z, c)


def along_second(k):
    return lambda x, y, z, c: (x, y + k, z, c) if c == 0 else (x + k, y, z, c)


def along_z(k):
    return lambda x, y, z, c: (x, y, z + k, c)


def apart(k):
    return lambda x, y, z, c: (x, y, z + k, c) if c == 0 else (x, y, z - k, c)


def across():
    groups = {}
    for y, zh, x, c, zl in np.ndindex(*SIZES):
        groups.setdefault((c, y if c else x), []).append(flat(x, y, zh * 4 + zl, c))
    return list(groups.values())


def swap(x, y, z, c):
    return (x, y, z, 1 - c)


def unit(rows):
    scale = jnp.sqrt(jnp.mean(rows * rows, axis=-1, keepdims=True) + 1e-06)
    return (rows / (scale * math.sqrt(rows.shape[-1]))).astype(jnp.bfloat16)


def text_unit_kernel(raw, out, kept):
    out[...] = unit(raw[...])
    kept[...] = out[...]


def image_unit_kernel(raw, text, text_far, out, kept, pair, pair_kept):
    out[...] = unit(raw[...])
    kept[...] = out[...]
    stack(pair, (text, text_far))
    stack(pair_kept, (text, text_far))


def stack(out, sources):
    row = 0
    for src in sources:
        out[row : row + src.shape[0], :] = src[...]
        row += src.shape[0]


def gather_kernel(i0, i1, i2, i3, own, pair, pair_2, after, cols_after, rows_after, line, message, hop, kept):
    stack(line, (i0, i1, i2, i3))
    stack(message, (pair, pair_2))
    hop[...] = pair_2[:48]
    stack(kept, (own, pair_2))


def ids_kernel(image, text, after, image_out, text_out):
    image_out[...] = image[...]
    text_out[...] = text[...]


def flag_kernel(*refs):
    refs[-1][...] = jnp.zeros_like(refs[-1])


def copy_kernel(src, after, out):
    out[...] = src[...]


def ride(out, row, value):
    high = value.astype(jnp.bfloat16).astype(jnp.float32)
    mid = (value - high).astype(jnp.bfloat16).astype(jnp.float32)
    low = value - high - mid
    at = lax.broadcasted_iota(jnp.int32, (16, 128), 0)
    extra = jnp.where(at == 0, high, jnp.where(at == 1, mid, jnp.where(at == 2, low, 0.0)))
    out[row:, :] = jnp.zeros((16, out.shape[1]), out.dtype)
    out[row:, :128] = extra.astype(out.dtype)


def alight(part, row):
    extra = part[row : row + 16, :128].astype(jnp.float32)
    return (extra[2:3] + extra[1:2]) + extra[0:1]


def terms_kernel(first, log_temp, bias, rows_id, cols_id, before, *refs):
    if first:
        pieces, (scaled, sums, text, image) = refs[:7], refs[7:]
        stack(text, pieces[:3])
        stack(image, pieces[3:])
        far = ()
    else:
        text, pieces, (*far, scaled, sums, image) = refs[0], refs[1:5], refs[5:]
        stack(image, pieces)
    temp = jnp.exp(jnp.full((1, 1), log_temp[0], jnp.float32))
    offset = bias[0]
    totals = [before[n] for n in range(3)]
    cols = cols_id[:, :768] if first else cols_id[:, 768:]
    rows = jnp.transpose(jnp.broadcast_to(rows_id[...].astype(jnp.float32), (128, 384)))[:, :1].astype(jnp.int32)
    for tile in range(2):
        at = slice(192 * tile, 192 * (tile + 1))
        cosine = lax.dot_general(
            text[at, :], image[...], (((1,), (1,)), ((), ())), preferred_element_type=jnp.float32
        )
        logits = temp * cosine + offset
        same = rows[at, :] == cols
        margin = jnp.where(same, -logits, logits)
        decay = jnp.exp(-jnp.abs(margin))
        inverse = 1.0 / (1.0 + decay)
        sigmoid = jnp.where(margin >= 0, inverse, decay * inverse)
        grad = jnp.where(same, -sigmoid, sigmoid)
        loss = jnp.maximum(margin, 0.0) + jnp.log1p(decay)
        scaled[at, :] = grad.astype(jnp.bfloat16)
        for n, value in enumerate((loss, grad, grad * cosine)):
            totals[n] = totals[n] + jnp.sum(value.reshape(24, 8, 768), axis=0)
    if not far:
        for n in range(3):
            sums[n] = totals[n]
        return
    lane = lax.broadcasted_iota(jnp.int32, (1, 128), 1)
    out = jnp.zeros((1, 128), jnp.float32)
    for n in range(3):
        out = jnp.where(lane == n, jnp.sum(totals[n]), out)
    sums[...] = jnp.broadcast_to(out, sums.shape)
    far[0][:768, :] = lax.dot_general(
        scaled[...], text[...], (((0,), (0,)), ((), ())), preferred_element_type=jnp.float32
    ).astype(jnp.bfloat16)
    ride(far[0], 768, out)


def text_kernel(scaled_own, scaled_far, image, image_far, own, pair, opposite, last):
    total = jnp.dot(scaled_own[...], image[...], preferred_element_type=jnp.float32)
    total = total + jnp.dot(scaled_far[...], image_far[...], preferred_element_type=jnp.float32)
    row = 0
    for dst in (own, pair, opposite, last):
        dst[...] = total[row : row + dst.shape[0]].astype(dst.dtype)
        row += dst.shape[0]


def image_kernel(scaled, sums, text, back, own, low1, low2, low3, sums_out):
    part = lax.dot_general(
        scaled[...], text[...], (((0,), (0,)), ((), ())), preferred_element_type=jnp.float32
    )
    for n, dst in enumerate((own, low1, low2, low3)):
        at = slice(192 * n, 192 * (n + 1))
        dst[...] = (part[at] + back[at].astype(jnp.float32)).astype(dst.dtype)
    sums_out[...] = jnp.broadcast_to((sums[...] + alight(back, 768))[None], sums_out.shape)


def near_kernel(own, pair, back, hop, out_own, out_far, low):
    out_own[...] = own[...] + back[:48].astype(jnp.float32)
    out_far[...] = back[48:96].astype(jnp.float32)
    total = pair[...] + back[96:].astype(jnp.float32)
    low[:48] = (total[:48] + hop[...].astype(jnp.float32)).astype(low.dtype)
    low[48:] = total[48:].astype(low.dtype)


def add_kernel(own, r1, r2, r3, terms, out_own, low1, low2, low3, sums):
    total = own[...] + r1[...].astype(jnp.float32) + r2[...].astype(jnp.float32) + r3[...].astype(jnp.float32)
    out_own[...] = total[:48]
    value = jnp.sum(terms[...], axis=0)
    sums[...] = value
    for n, dst in enumerate((low1, low2, low3), 1):
        dst[:48, :] = total[48 * n : 48 * (n + 1)].astype(dst.dtype)
        ride(dst, 48, value[:1])


def far_kernel(own, far, back, after, out_own, low):
    out_own[...] = own[...] + back[:48].astype(jnp.float32)
    low[...] = (far[...] + back[48:].astype(jnp.float32)).astype(low.dtype)


def finish_kernel(log_temp, image_raw, image_own, i1, i2, i3, text_raw, text_own, t1, sums,
                  image_out, text_out, loss, bias_grad, temp_grad):
    temp = jnp.exp(jnp.full((1, 1), log_temp[0], jnp.float32))
    for raw, own, parts, out in (
        (image_raw, image_own, (i1, i2, i3), image_out), (text_raw, text_own, (t1,), text_out),
    ):
        rows = raw[...]
        width = rows.shape[-1]
        grad = own[...]
        for part in parts:
            grad = grad + part[:48].astype(jnp.float32)
        grad = grad * temp
        square = jnp.mean(rows * rows, axis=-1, keepdims=True) + 1e-06
        inner = jnp.sum(rows * grad, axis=-1, keepdims=True)
        out[...] = (grad - rows * (inner / (square * width))) / (jnp.sqrt(square) * math.sqrt(width))
    values = [sums[0:1]] + [alight(part, 48) for part in (i1, i2, i3)]
    total = (values[0] + values[3]) + (values[1] + values[2])
    lane = lax.broadcasted_iota(jnp.int32, total.shape, 1)
    for n, (out, factor) in enumerate(((loss, 1.0), (bias_grad, 1.0), (temp_grad, temp))):
        out[0] = jnp.sum(jnp.where(lane == n, total * factor, 0.0)) / (48 * 256)


def i32(*shape):
    return jax.ShapeDtypeStruct(shape, jnp.int32)


def f32(*shape):
    return jax.ShapeDtypeStruct(shape, jnp.float32)


def b16(*shape):
    return jax.ShapeDtypeStruct(shape, jnp.bfloat16)


def local(kernel, out_shape, *args, after=(), scratch=(), grant=8):
    return pl.pallas_call(
        kernel,
        out_shape=out_shape,
        in_specs=[SMEM if a.shape == (1,) else VMEM for a in args] + [ANY] * len(after),
        out_specs=tuple(SMEM if o.shape == (1,) else VMEM for o in out_shape),
        scratch_shapes=list(scratch),
        compiler_params=pltpu.CompilerParams(vmem_limit_bytes=grant * 1024 * 1024),
    )(*args, *after)


def body(image_raw, text_raw, image_ids, text_ids, log_temp, bias):
    pairs, width = image_raw.shape
    x, y, c = lax.axis_index("x"), lax.axis_index("y"), lax.axis_index("core")
    z = lax.axis_index("zh") * 4 + lax.axis_index("zl")
    back = (0,) + OFFSETS
    cols_from = []
    for core in (c, 1 - c):
        for k in back:
            for j in back:
                sx = jnp.where(core == 0, x - j, x - k) % 4
                sy = jnp.where(core == 0, y - k, y - j) % 4
                cols_from.append(flat(sx, sy, z, core))
    step = jnp.where(c == 0, 1, -1)
    rows_from = [flat(x, y, z, c)]
    for k in (2, 4, 1, 3):
        rows_from += [flat(x, y, (z - k * step) % 8, core) for core in ((c,) if k == 4 else (c, 1 - c))]

    text_unit, text_kept = local(text_unit_kernel, (b16(pairs, width),) * 2, text_raw)
    image_unit, image_kept, pair, pair_kept = local(
        image_unit_kernel, (b16(pairs, width),) * 2 + (b16(2 * pairs, width),) * 2,
        image_raw, text_kept, send(text_unit, swap, "pair"),
    )

    parts = [send(image_unit, along_first(k), "first") for k in OFFSETS]
    pair_2 = send(pair, apart(2), "z2")
    image_ids, text_ids = local(ids_kernel, (i32(256, pairs),) * 2, image_ids.reshape(256, pairs), text_ids.reshape(256, pairs), after=parts[1:2])
    cols_id = image_ids.reshape(256, pairs)[jnp.stack(cols_from)].reshape(1, 32 * pairs)
    rows_id = text_ids.reshape(256, pairs)[jnp.stack(rows_from)].reshape(1, 8 * pairs)
    (flag,) = local(flag_kernel, (f32(8, 128),), after=parts)
    flag = send(flag, swap, "flag")
    line, message, hop, kept = local(
        gather_kernel, (b16(4 * pairs, width),) * 2 + (b16(pairs, width), b16(3 * pairs, width)),
        image_kept, *parts, text_kept, pair_kept, pair_2, after=(flag, cols_id, rows_id),
    )

    plane = [line] + [send(line, along_second(k), "second") for k in OFFSETS]
    text = (kept, send(hop, apart(2), "z4"), send(message, apart(1), "z1"))
    (line_kept,) = local(copy_kernel, (b16(4 * pairs, width),), line, after=(plane[1],))
    plane_far = [send(p, swap, "swap") for p in [line_kept] + plane[1:]]

    scaled_own, sums, text, image = local(
        functools.partial(terms_kernel, True),
        (b16(384, 768), f32(3, 8, 768), b16(384, width), b16(768, width)),
        log_temp, bias, rows_id, cols_id, jnp.zeros((3, 8, 768), jnp.float32), *text, *plane, grant=16,
    )
    far, scaled_far, sums, image_far = local(
        functools.partial(terms_kernel, False),
        (b16(784, width), b16(384, 768), f32(8, 128), b16(768, width)),
        log_temp, bias, rows_id, cols_id, sums, text, *plane_far, grant=16,
    )
    back = send(far, swap, "rswap")
    text_own, text_pair, hop, last = local(
        text_kernel, (f32(pairs, width), f32(2 * pairs, width), b16(pairs, width), b16(4 * pairs, width)),
        scaled_own, scaled_far, image, image_far, grant=16,
    )
    last = send(last, apart(-1), "rz1")
    hop = send(hop, apart(-2), "rz4")
    image_own, *lows, spread = local(
        image_kernel, (f32(192, width),) + (b16(192, width),) * 3 + (f32(32, 8, 128),),
        scaled_own, sums, text, back, grant=16,
    )
    image_parts = [send(p, along_second(-k), "rsecond") for p, k in zip(lows, OFFSETS)]
    text_own, text_far, low = local(
        near_kernel, (f32(pairs, width), f32(pairs, width), b16(2 * pairs, width)),
        text_own, text_pair, last, hop,
    )
    back = send(low, apart(-2), "rz2")
    with jax.named_scope("terms"):
        spread = lax.all_to_all(spread, AXES, 0, 0, tiled=True, axis_index_groups=across())
    image_own, *lows, sums = local(
        add_kernel, (f32(pairs, width),) + (b16(pairs + 16, width),) * 3 + (f32(8, 128),),
        image_own, *image_parts, spread,
    )
    image_parts = [send(p, along_first(-k), "rfirst") for p, k in zip(lows, OFFSETS)]
    text_own, far_low = local(
        far_kernel, (f32(pairs, width), b16(pairs, width)), text_own, text_far, back, after=(image_own,),
    )
    image_grad, text_grad, loss, bias_grad, temp_grad = local(
        finish_kernel, (f32(pairs, width),) * 2 + (f32(1),) * 3,
        log_temp, image_raw, image_own, *image_parts, text_raw, text_own, send(far_low, swap, "rpair"), sums,
    )
    return (loss, image_grad, text_grad, temp_grad, bias_grad)


def solution(mesh):
    fine = Mesh(mesh.devices.reshape(SIZES), AXES)
    rows = P(AXES, None)
    return jax.shard_map(
        body,
        mesh=fine,
        in_specs=(rows, rows, P(), P(), P(), P()),
        out_specs=(P(), rows, rows, P(), P()),
        check_vma=False,
    )
```

```python
import functools
import math

import jax
import jax.numpy as jnp
import numpy as np
from jax import lax
from jax.experimental import pallas as pl
from jax.experimental.pallas import tpu as pltpu
from jax.sharding import Mesh
from jax.sharding import PartitionSpec as P

SIZES = (4, 2, 4, 2, 4)
AXES = ("y", "zh", "x", "core", "zl")
ROWS = 48
OFFSETS = (1, 3, 2)
ANY = pl.BlockSpec(memory_space=pl.ANY)
VMEM = pl.BlockSpec(memory_space=pltpu.VMEM)
SMEM = pl.BlockSpec(memory_space=pltpu.SMEM)


def flat(x, y, z, c):
    return (((y * 2 + z // 4) * 4 + x) * 2 + c) * 4 + z % 4


def send(value, where, name="move"):
    pairs = []
    for y, zh, x, c, zl in np.ndindex(*SIZES):
        z = zh * 4 + zl
        tx, ty, tz, tc = where(x, y, z, c)
        pairs.append((flat(x, y, z, c), flat(tx % 4, ty % 4, tz % 8, tc % 2)))
    with jax.named_scope(name):
        return lax.ppermute(value, AXES, pairs)


def along_first(k):
    return lambda x, y, z, c: (x + k, y, z, c) if c == 0 else (x, y + k, z, c)


def along_second(k):
    return lambda x, y, z, c: (x, y + k, z, c) if c == 0 else (x + k, y, z, c)


def along_z(k):
    return lambda x, y, z, c: (x, y, z + k, c)


def apart(k):
    return lambda x, y, z, c: (x, y, z + k, c) if c == 0 else (x, y, z - k, c)


def across():
    groups = {}
    for y, zh, x, c, zl in np.ndindex(*SIZES):
        groups.setdefault((c, y if c else x), []).append(flat(x, y, zh * 4 + zl, c))
    return list(groups.values())


def swap(x, y, z, c):
    return (x, y, z, 1 - c)


def unit(rows):
    scale = jnp.sqrt(jnp.mean(rows * rows, axis=-1, keepdims=True) + 1e-06)
    return (rows / (scale * math.sqrt(rows.shape[-1]))).astype(jnp.bfloat16)


def text_unit_kernel(raw, out, kept):
    out[...] = unit(raw[...])
    kept[...] = out[...]


def image_unit_kernel(raw, text, text_far, out, kept, pair, pair_kept):
    out[...] = unit(raw[...])
    kept[...] = out[...]
    stack(pair, (text, text_far))
    stack(pair_kept, (text, text_far))


def stack(out, sources):
    row = 0
    for src in sources:
        out[row : row + src.shape[0], :] = src[...]
        row += src.shape[0]


def gather_kernel(i0, i1, i2, i3, own, pair, pair_2, after, cols_after, rows_after, line, message, hop, kept):
    stack(line, (i0, i1, i2, i3))
    stack(message, (pair, pair_2))
    hop[...] = pair_2[:48]
    stack(kept, (own, pair_2))


def ids_kernel(image, text, after, image_out, text_out):
    image_out[...] = image[...]
    text_out[...] = text[...]


def flag_kernel(*refs):
    refs[-1][...] = jnp.zeros_like(refs[-1])


def copy_kernel(src, after, out):
    out[...] = src[...]


def ride(out, row, value):
    high = value.astype(jnp.bfloat16).astype(jnp.float32)
    mid = (value - high).astype(jnp.bfloat16).astype(jnp.float32)
    low = value - high - mid
    at = lax.broadcasted_iota(jnp.int32, (16, 128), 0)
    extra = jnp.where(at == 0, high, jnp.where(at == 1, mid, jnp.where(at == 2, low, 0.0)))
    out[row:, :] = jnp.zeros((16, out.shape[1]), out.dtype)
    out[row:, :128] = extra.astype(out.dtype)


def alight(part, row):
    extra = part[row : row + 16, :128].astype(jnp.float32)
    return (extra[2:3] + extra[1:2]) + extra[0:1]


def terms_kernel(first, log_temp, bias, rows_id, cols_id, before, *refs):
    if first:
        pieces, (scaled, sums, text, image) = refs[:7], refs[7:]
        stack(text, pieces[:3])
        stack(image, pieces[3:])
        far = ()
    else:
        text, pieces, (*far, scaled, sums, image) = refs[0], refs[1:5], refs[5:]
        stack(image, pieces)
    temp = jnp.exp(jnp.full((1, 1), log_temp[0], jnp.float32))
    offset = bias[0]
    totals = [before[n] for n in range(3)]
    cols = cols_id[:, :768] if first else cols_id[:, 768:]
    rows = jnp.transpose(jnp.broadcast_to(rows_id[...].astype(jnp.float32), (128, 384)))[:, :1].astype(jnp.int32)
    for tile in range(2):
        at = slice(192 * tile, 192 * (tile + 1))
        cosine = lax.dot_general(
            text[at, :], image[...], (((1,), (1,)), ((), ())), preferred_element_type=jnp.float32
        )
        logits = temp * cosine + offset
        same = rows[at, :] == cols
        margin = jnp.where(same, -logits, logits)
        decay = jnp.exp(-jnp.abs(margin))
        inverse = 1.0 / (1.0 + decay)
        sigmoid = jnp.where(margin >= 0, inverse, decay * inverse)
        grad = jnp.where(same, -sigmoid, sigmoid)
        loss = jnp.maximum(margin, 0.0) + jnp.log1p(decay)
        scaled[at, :] = grad.astype(jnp.bfloat16)
        for n, value in enumerate((loss, grad, grad * cosine)):
            totals[n] = totals[n] + jnp.sum(value.reshape(24, 8, 768), axis=0)
    if not far:
        for n in range(3):
            sums[n] = totals[n]
        return
    lane = lax.broadcasted_iota(jnp.int32, (1, 128), 1)
    out = jnp.zeros((1, 128), jnp.float32)
    for n in range(3):
        out = jnp.where(lane == n, jnp.sum(totals[n]), out)
    sums[...] = jnp.broadcast_to(out, sums.shape)
    far[0][:768, :] = lax.dot_general(
        scaled[...], text[...], (((0,), (0,)), ((), ())), preferred_element_type=jnp.float32
    ).astype(jnp.bfloat16)
    ride(far[0], 768, out)


def text_kernel(scaled_own, scaled_far, image, image_far, own, pair, opposite, last):
    total = jnp.dot(scaled_own[...], image[...], preferred_element_type=jnp.float32)
    total = total + jnp.dot(scaled_far[...], image_far[...], preferred_element_type=jnp.float32)
    row = 0
    for dst in (own, pair, opposite, last):
        dst[...] = total[row : row + dst.shape[0]].astype(dst.dtype)
        row += dst.shape[0]


def image_kernel(scaled, sums, text, back, own, low1, low2, low3, sums_out):
    part = lax.dot_general(
        scaled[...], text[...], (((0,), (0,)), ((), ())), preferred_element_type=jnp.float32
    )
    for n, dst in enumerate((own, low1, low2, low3)):
        at = slice(192 * n, 192 * (n + 1))
        dst[...] = (part[at] + back[at].astype(jnp.float32)).astype(dst.dtype)
    sums_out[...] = jnp.broadcast_to((sums[...] + alight(back, 768))[None], sums_out.shape)


def near_kernel(own, pair, back, hop, out_own, out_far, low):
    out_own[...] = own[...] + back[:48].astype(jnp.float32)
    out_far[...] = back[48:96].astype(jnp.float32)
    total = pair[...] + back[96:].astype(jnp.float32)
    low[:48] = (total[:48] + hop[...].astype(jnp.float32)).astype(low.dtype)
    low[48:] = total[48:].astype(low.dtype)


def add_kernel(own, r1, r2, r3, terms, out_own, low1, low2, low3, sums):
    total = own[...] + r1[...].astype(jnp.float32) + r2[...].astype(jnp.float32) + r3[...].astype(jnp.float32)
    out_own[...] = total[:48]
    value = jnp.sum(terms[...], axis=0)
    sums[...] = value
    for n, dst in enumerate((low1, low2, low3), 1):
        dst[:48, :] = total[48 * n : 48 * (n + 1)].astype(dst.dtype)
        ride(dst, 48, value[:1])


def far_kernel(own, far, back, after, out_own, low):
    out_own[...] = own[...] + back[:48].astype(jnp.float32)
    low[...] = (far[...] + back[48:].astype(jnp.float32)).astype(low.dtype)


def finish_kernel(log_temp, image_raw, image_own, i1, i2, i3, text_raw, text_own, t1, sums,
                  image_out, text_out, loss, bias_grad, temp_grad):
    temp = jnp.exp(jnp.full((1, 1), log_temp[0], jnp.float32))
    for raw, own, parts, out in (
        (image_raw, image_own, (i1, i2, i3), image_out), (text_raw, text_own, (t1,), text_out),
    ):
        rows = raw[...]
        width = rows.shape[-1]
        grad = own[...]
        for part in parts:
            grad = grad + part[:48].astype(jnp.float32)
        grad = grad * temp
        square = jnp.mean(rows * rows, axis=-1, keepdims=True) + 1e-06
        inner = jnp.sum(rows * grad, axis=-1, keepdims=True)
        out[...] = (grad - rows * (inner / (square * width))) / (jnp.sqrt(square) * math.sqrt(width))
    values = [sums[0:1]] + [alight(part, 48) for part in (i1, i2, i3)]
    total = (values[0] + values[3]) + (values[1] + values[2])
    lane = lax.broadcasted_iota(jnp.int32, total.shape, 1)
    for n, (out, factor) in enumerate(((loss, 1.0), (bias_grad, 1.0), (temp_grad, temp))):
        out[0] = jnp.sum(jnp.where(lane == n, total * factor, 0.0)) / (48 * 256)


def i32(*shape):
    return jax.ShapeDtypeStruct(shape, jnp.int32)


def f32(*shape):
    return jax.ShapeDtypeStruct(shape, jnp.float32)


def b16(*shape):
    return jax.ShapeDtypeStruct(shape, jnp.bfloat16)


def local(kernel, out_shape, *args, after=(), scratch=(), grant=4):
    return pl.pallas_call(
        kernel,
        out_shape=out_shape,
        in_specs=[SMEM if a.shape == (1,) else VMEM for a in args] + [ANY] * len(after),
        out_specs=tuple(SMEM if o.shape == (1,) else VMEM for o in out_shape),
        scratch_shapes=list(scratch),
        compiler_params=pltpu.CompilerParams(vmem_limit_bytes=grant * 1024 * 1024),
    )(*args, *after)


def body(image_raw, text_raw, image_ids, text_ids, log_temp, bias):
    pairs, width = image_raw.shape
    x, y, c = lax.axis_index("x"), lax.axis_index("y"), lax.axis_index("core")
    z = lax.axis_index("zh") * 4 + lax.axis_index("zl")
    back = (0,) + OFFSETS
    cols_from = []
    for core in (c, 1 - c):
        for k in back:
            for j in back:
                sx = jnp.where(core == 0, x - j, x - k) % 4
                sy = jnp.where(core == 0, y - k, y - j) % 4
                cols_from.append(flat(sx, sy, z, core))
    step = jnp.where(c == 0, 1, -1)
    rows_from = [flat(x, y, z, c)]
    for k in (2, 4, 1, 3):
        rows_from += [flat(x, y, (z - k * step) % 8, core) for core in ((c,) if k == 4 else (c, 1 - c))]

    text_unit, text_kept = local(text_unit_kernel, (b16(pairs, width),) * 2, text_raw)
    image_unit, image_kept, pair, pair_kept = local(
        image_unit_kernel, (b16(pairs, width),) * 2 + (b16(2 * pairs, width),) * 2,
        image_raw, text_kept, send(text_unit, swap, "pair"),
    )

    parts = [send(image_unit, along_first(k), "first") for k in OFFSETS]
    pair_2 = send(pair, apart(2), "z2")
    image_ids, text_ids = local(ids_kernel, (i32(256, pairs),) * 2, image_ids.reshape(256, pairs), text_ids.reshape(256, pairs), after=parts[2:3])
    cols_id = image_ids.reshape(256, pairs)[jnp.stack(cols_from)].reshape(1, 32 * pairs)
    rows_id = text_ids.reshape(256, pairs)[jnp.stack(rows_from)].reshape(1, 8 * pairs)
    (flag,) = local(flag_kernel, (f32(8, 128),), after=parts)
    flag = send(flag, swap, "flag")
    line, message, hop, kept = local(
        gather_kernel, (b16(4 * pairs, width),) * 2 + (b16(pairs, width), b16(3 * pairs, width)),
        image_kept, *parts, text_kept, pair_kept, pair_2, after=(flag, cols_id, rows_id),
    )

    plane = [line] + [send(line, along_second(k), "second") for k in OFFSETS]
    text = (kept, send(hop, apart(2), "z4"), send(message, apart(1), "z1"))
    (line_kept,) = local(copy_kernel, (b16(4 * pairs, width),), line, after=(plane[1],))
    plane_far = [send(p, swap, "swap") for p in [line_kept] + plane[1:]]

    scaled_own, sums, text, image = local(
        functools.partial(terms_kernel, True),
        (b16(384, 768), f32(3, 8, 768), b16(384, width), b16(768, width)),
        log_temp, bias, rows_id, cols_id, jnp.zeros((3, 8, 768), jnp.float32), *text, *plane, grant=12,
    )
    far, scaled_far, sums, image_far = local(
        functools.partial(terms_kernel, False),
        (b16(784, width), b16(384, 768), f32(8, 128), b16(768, width)),
        log_temp, bias, rows_id, cols_id, sums, text, *plane_far, grant=12,
    )
    back = send(far, swap, "rswap")
    text_own, text_pair, hop, last = local(
        text_kernel, (f32(pairs, width), f32(2 * pairs, width), b16(pairs, width), b16(4 * pairs, width)),
        scaled_own, scaled_far, image, image_far, grant=12,
    )
    last = send(last, apart(-1), "rz1")
    hop = send(hop, apart(-2), "rz4")
    image_own, *lows, spread = local(
        image_kernel, (f32(192, width),) + (b16(192, width),) * 3 + (f32(32, 8, 128),),
        scaled_own, sums, text, back, grant=12,
    )
    image_parts = [send(p, along_second(-k), "rsecond") for p, k in zip(lows, OFFSETS)]
    text_own, text_far, low = local(
        near_kernel, (f32(pairs, width), f32(pairs, width), b16(2 * pairs, width)),
        text_own, text_pair, last, hop,
    )
    back = send(low, apart(-2), "rz2")
    with jax.named_scope("terms"):
        spread = lax.all_to_all(spread, AXES, 0, 0, tiled=True, axis_index_groups=across())
    image_own, *lows, sums = local(
        add_kernel, (f32(pairs, width),) + (b16(pairs + 16, width),) * 3 + (f32(8, 128),),
        image_own, *image_parts, spread,
    )
    image_parts = [send(p, along_first(-k), "rfirst") for p, k in zip(lows, OFFSETS)]
    text_own, far_low = local(
        far_kernel, (f32(pairs, width), b16(pairs, width)), text_own, text_far, back, after=(image_own,),
    )
    image_grad, text_grad, loss, bias_grad, temp_grad = local(
        finish_kernel, (f32(pairs, width),) * 2 + (f32(1),) * 3,
        log_temp, image_raw, image_own, *image_parts, text_raw, text_own, send(far_low, swap, "rpair"), sums,
    )
    return (loss, image_grad, text_grad, temp_grad, bias_grad)


def solution(mesh):
    fine = Mesh(mesh.devices.reshape(SIZES), AXES)
    rows = P(AXES, None)
    return jax.shard_map(
        body,
        mesh=fine,
        in_specs=(rows, rows, P(), P(), P(), P()),
        out_specs=(P(), rows, rows, P(), P()),
        check_vma=False,
    )
```

```python
import functools
import math

import jax
import jax.numpy as jnp
import numpy as np
from jax import lax
from jax.experimental import pallas as pl
from jax.experimental.pallas import tpu as pltpu
from jax.sharding import Mesh
from jax.sharding import PartitionSpec as P

SIZES = (4, 2, 4, 2, 4)
AXES = ("y", "zh", "x", "core", "zl")
ROWS = 48
OFFSETS = (1, 3, 2)
ANY = pl.BlockSpec(memory_space=pl.ANY)
VMEM = pl.BlockSpec(memory_space=pltpu.VMEM)
SMEM = pl.BlockSpec(memory_space=pltpu.SMEM)


def flat(x, y, z, c):
    return (((y * 2 + z // 4) * 4 + x) * 2 + c) * 4 + z % 4


def send(value, where, name="move"):
    pairs = []
    for y, zh, x, c, zl in np.ndindex(*SIZES):
        z = zh * 4 + zl
        tx, ty, tz, tc = where(x, y, z, c)
        pairs.append((flat(x, y, z, c), flat(tx % 4, ty % 4, tz % 8, tc % 2)))
    with jax.named_scope(name):
        return lax.ppermute(value, AXES, pairs)


def along_first(k):
    return lambda x, y, z, c: (x + k, y, z, c) if c == 0 else (x, y + k, z, c)


def along_second(k):
    return lambda x, y, z, c: (x, y + k, z, c) if c == 0 else (x + k, y, z, c)


def along_z(k):
    return lambda x, y, z, c: (x, y, z + k, c)


def apart(k):
    return lambda x, y, z, c: (x, y, z + k, c) if c == 0 else (x, y, z - k, c)


def across():
    groups = {}
    for y, zh, x, c, zl in np.ndindex(*SIZES):
        groups.setdefault((c, y if c else x), []).append(flat(x, y, zh * 4 + zl, c))
    return list(groups.values())


def swap(x, y, z, c):
    return (x, y, z, 1 - c)


def unit(rows):
    scale = jnp.sqrt(jnp.mean(rows * rows, axis=-1, keepdims=True) + 1e-06)
    return (rows / (scale * math.sqrt(rows.shape[-1]))).astype(jnp.bfloat16)


def text_unit_kernel(raw, out, kept):
    out[...] = unit(raw[...])
    kept[...] = out[...]


def image_unit_kernel(raw, text, text_far, out, kept, pair, pair_kept):
    out[...] = unit(raw[...])
    kept[...] = out[...]
    stack(pair, (text, text_far))
    stack(pair_kept, (text, text_far))


def stack(out, sources):
    row = 0
    for src in sources:
        out[row : row + src.shape[0], :] = src[...]
        row += src.shape[0]


def gather_kernel(i0, i1, i2, i3, own, pair, pair_2, after, cols_after, rows_after, line, message, hop, kept):
    stack(line, (i0, i1, i2, i3))
    stack(message, (pair, pair_2))
    hop[...] = pair_2[:48]
    stack(kept, (own, pair_2))


def ids_kernel(image, text, after, image_out, text_out):
    image_out[...] = image[...]
    text_out[...] = text[...]


def flag_kernel(*refs):
    refs[-1][...] = jnp.zeros_like(refs[-1])


def copy_kernel(src, after, out):
    out[...] = src[...]


def ride(out, row, value):
    high = value.astype(jnp.bfloat16).astype(jnp.float32)
    mid = (value - high).astype(jnp.bfloat16).astype(jnp.float32)
    low = value - high - mid
    at = lax.broadcasted_iota(jnp.int32, (16, 128), 0)
    extra = jnp.where(at == 0, high, jnp.where(at == 1, mid, jnp.where(at == 2, low, 0.0)))
    out[row:, :] = jnp.zeros((16, out.shape[1]), out.dtype)
    out[row:, :128] = extra.astype(out.dtype)


def alight(part, row):
    extra = part[row : row + 16, :128].astype(jnp.float32)
    return (extra[2:3] + extra[1:2]) + extra[0:1]


def terms_kernel(first, log_temp, bias, rows_id, cols_id, before, *refs):
    if first:
        pieces, (scaled, sums, text, image) = refs[:7], refs[7:]
        stack(text, pieces[:3])
        stack(image, (pieces[3], pieces[5], pieces[6], pieces[4]))
        far = ()
    else:
        text, pieces, (*far, scaled, sums, image) = refs[0], refs[1:5], refs[5:]
        stack(image, pieces)
    temp = jnp.exp(jnp.full((1, 1), log_temp[0], jnp.float32))
    offset = bias[0]
    totals = [before[n] for n in range(3)]
    cols = cols_id[:, :768] if first else cols_id[:, 768:]
    rows = jnp.transpose(jnp.broadcast_to(rows_id[...].astype(jnp.float32), (128, 384)))[:, :1].astype(jnp.int32)
    for tile in range(2):
        at = slice(192 * tile, 192 * (tile + 1))
        cosine = lax.dot_general(
            text[at, :], image[...], (((1,), (1,)), ((), ())), preferred_element_type=jnp.float32
        )
        logits = temp * cosine + offset
        same = rows[at, :] == cols
        margin = jnp.where(same, -logits, logits)
        decay = jnp.exp(-jnp.abs(margin))
        inverse = 1.0 / (1.0 + decay)
        sigmoid = jnp.where(margin >= 0, inverse, decay * inverse)
        grad = jnp.where(same, -sigmoid, sigmoid)
        loss = jnp.maximum(margin, 0.0) + jnp.log1p(decay)
        scaled[at, :] = grad.astype(jnp.bfloat16)
        for n, value in enumerate((loss, grad, grad * cosine)):
            totals[n] = totals[n] + jnp.sum(value.reshape(24, 8, 768), axis=0)
    if not far:
        for n in range(3):
            sums[n] = totals[n]
        return
    lane = lax.broadcasted_iota(jnp.int32, (1, 128), 1)
    out = jnp.zeros((1, 128), jnp.float32)
    for n in range(3):
        out = jnp.where(lane == n, jnp.sum(totals[n]), out)
    sums[...] = jnp.broadcast_to(out, sums.shape)
    far[0][:768, :] = lax.dot_general(
        scaled[...], text[...], (((0,), (0,)), ((), ())), preferred_element_type=jnp.float32
    ).astype(jnp.bfloat16)
    ride(far[0], 768, out)


def text_kernel(scaled_own, scaled_far, image, image_far, own, pair, opposite, last):
    total = jnp.dot(scaled_own[...], image[...], preferred_element_type=jnp.float32)
    total = total + jnp.dot(scaled_far[...], image_far[...], preferred_element_type=jnp.float32)
    row = 0
    for dst in (own, pair, opposite, last):
        dst[...] = total[row : row + dst.shape[0]].astype(dst.dtype)
        row += dst.shape[0]


def image_kernel(scaled, sums, text, back, own, low1, low2, low3, sums_out):
    part = lax.dot_general(
        scaled[...], text[...], (((0,), (0,)), ((), ())), preferred_element_type=jnp.float32
    )
    for n, dst in enumerate((own, low1, low2, low3)):
        at = slice(192 * n, 192 * (n + 1))
        dst[...] = (part[at] + back[at].astype(jnp.float32)).astype(dst.dtype)
    sums_out[...] = jnp.broadcast_to((sums[...] + alight(back, 768))[None], sums_out.shape)


def near_kernel(own, pair, back, hop, out_own, out_far, low):
    out_own[...] = own[...] + back[:48].astype(jnp.float32)
    out_far[...] = back[48:96].astype(jnp.float32)
    total = pair[...] + back[96:].astype(jnp.float32)
    low[:48] = (total[:48] + hop[...].astype(jnp.float32)).astype(low.dtype)
    low[48:] = total[48:].astype(low.dtype)


def add_kernel(own, r1, r2, r3, terms, out_own, low1, low2, low3, sums):
    total = own[...] + r1[...].astype(jnp.float32) + r2[...].astype(jnp.float32) + r3[...].astype(jnp.float32)
    out_own[...] = total[:48]
    value = jnp.sum(terms[...], axis=0)
    sums[...] = value
    for n, dst in enumerate((low1, low2, low3), 1):
        dst[:48, :] = total[48 * n : 48 * (n + 1)].astype(dst.dtype)
        ride(dst, 48, value[:1])


def far_kernel(own, far, back, after, out_own, low):
    out_own[...] = own[...] + back[:48].astype(jnp.float32)
    low[...] = (far[...] + back[48:].astype(jnp.float32)).astype(low.dtype)


def finish_kernel(log_temp, image_raw, image_own, i1, i2, i3, text_raw, text_own, t1, sums,
                  image_out, text_out, loss, bias_grad, temp_grad):
    temp = jnp.exp(jnp.full((1, 1), log_temp[0], jnp.float32))
    for raw, own, parts, out in (
        (image_raw, image_own, (i1, i2, i3), image_out), (text_raw, text_own, (t1,), text_out),
    ):
        rows = raw[...]
        width = rows.shape[-1]
        grad = own[...]
        for part in parts:
            grad = grad + part[:48].astype(jnp.float32)
        grad = grad * temp
        square = jnp.mean(rows * rows, axis=-1, keepdims=True) + 1e-06
        inner = jnp.sum(rows * grad, axis=-1, keepdims=True)
        out[...] = (grad - rows * (inner / (square * width))) / (jnp.sqrt(square) * math.sqrt(width))
    values = [sums[0:1]] + [alight(part, 48) for part in (i1, i2, i3)]
    total = (values[0] + values[3]) + (values[1] + values[2])
    lane = lax.broadcasted_iota(jnp.int32, total.shape, 1)
    for n, (out, factor) in enumerate(((loss, 1.0), (bias_grad, 1.0), (temp_grad, temp))):
        out[0] = jnp.sum(jnp.where(lane == n, total * factor, 0.0)) / (48 * 256)


def i32(*shape):
    return jax.ShapeDtypeStruct(shape, jnp.int32)


def f32(*shape):
    return jax.ShapeDtypeStruct(shape, jnp.float32)


def b16(*shape):
    return jax.ShapeDtypeStruct(shape, jnp.bfloat16)


def local(kernel, out_shape, *args, after=(), scratch=(), grant=4):
    return pl.pallas_call(
        kernel,
        out_shape=out_shape,
        in_specs=[SMEM if a.shape == (1,) else VMEM for a in args] + [ANY] * len(after),
        out_specs=tuple(SMEM if o.shape == (1,) else VMEM for o in out_shape),
        scratch_shapes=list(scratch),
        compiler_params=pltpu.CompilerParams(vmem_limit_bytes=grant * 1024 * 1024),
    )(*args, *after)


def body(image_raw, text_raw, image_ids, text_ids, log_temp, bias):
    pairs, width = image_raw.shape
    x, y, c = lax.axis_index("x"), lax.axis_index("y"), lax.axis_index("core")
    z = lax.axis_index("zh") * 4 + lax.axis_index("zl")
    back = (0,) + OFFSETS
    cols_from = []
    for core in (c, 1 - c):
        for k in back:
            for j in back:
                sx = jnp.where(core == 0, x - j, x - k) % 4
                sy = jnp.where(core == 0, y - k, y - j) % 4
                cols_from.append(flat(sx, sy, z, core))
    step = jnp.where(c == 0, 1, -1)
    rows_from = [flat(x, y, z, c)]
    for k in (2, 4, 1, 3):
        rows_from += [flat(x, y, (z - k * step) % 8, core) for core in ((c,) if k == 4 else (c, 1 - c))]

    text_unit, text_kept = local(text_unit_kernel, (b16(pairs, width),) * 2, text_raw)
    image_unit, image_kept, pair, pair_kept = local(
        image_unit_kernel, (b16(pairs, width),) * 2 + (b16(2 * pairs, width),) * 2,
        image_raw, text_kept, send(text_unit, swap, "pair"),
    )

    parts = [send(image_unit, along_first(k), "first") for k in OFFSETS]
    pair_2 = send(pair, apart(2), "z2")
    image_ids, text_ids = local(ids_kernel, (i32(256, pairs),) * 2, image_ids.reshape(256, pairs), text_ids.reshape(256, pairs), after=parts[2:3])
    cols_id = image_ids.reshape(256, pairs)[jnp.stack(cols_from)].reshape(1, 32 * pairs)
    rows_id = text_ids.reshape(256, pairs)[jnp.stack(rows_from)].reshape(1, 8 * pairs)
    (flag,) = local(flag_kernel, (f32(8, 128),), after=parts)
    flag = send(flag, swap, "flag")
    line, message, hop, kept = local(
        gather_kernel, (b16(4 * pairs, width),) * 2 + (b16(pairs, width), b16(3 * pairs, width)),
        image_kept, *parts, text_kept, pair_kept, pair_2, after=(flag, cols_id, rows_id),
    )

    plane = [line] + [send(line, along_second(k), "second") for k in OFFSETS]
    text = (kept, send(hop, apart(2), "z4"), send(message, apart(1), "z1"))
    (line_kept,) = local(copy_kernel, (b16(4 * pairs, width),), line, after=(plane[1],))
    plane_far = [send(p, swap, "swap") for p in [line_kept] + plane[1:]]

    scaled_own, sums, text, image = local(
        functools.partial(terms_kernel, True),
        (b16(384, 768), f32(3, 8, 768), b16(384, width), b16(768, width)),
        log_temp, bias, rows_id, cols_id, jnp.zeros((3, 8, 768), jnp.float32), *text, plane[0], plane[3], *plane[1:3], grant=12,
    )
    far, scaled_far, sums, image_far = local(
        functools.partial(terms_kernel, False),
        (b16(784, width), b16(384, 768), f32(8, 128), b16(768, width)),
        log_temp, bias, rows_id, cols_id, sums, text, *plane_far, grant=12,
    )
    back = send(far, swap, "rswap")
    text_own, text_pair, hop, last = local(
        text_kernel, (f32(pairs, width), f32(2 * pairs, width), b16(pairs, width), b16(4 * pairs, width)),
        scaled_own, scaled_far, image, image_far, grant=12,
    )
    last = send(last, apart(-1), "rz1")
    hop = send(hop, apart(-2), "rz4")
    image_own, *lows, spread = local(
        image_kernel, (f32(192, width),) + (b16(192, width),) * 3 + (f32(32, 8, 128),),
        scaled_own, sums, text, back, grant=12,
    )
    image_parts = [send(p, along_second(-k), "rsecond") for p, k in zip(lows, OFFSETS)]
    text_own, text_far, low = local(
        near_kernel, (f32(pairs, width), f32(pairs, width), b16(2 * pairs, width)),
        text_own, text_pair, last, hop,
    )
    back = send(low, apart(-2), "rz2")
    with jax.named_scope("terms"):
        spread = lax.all_to_all(spread, AXES, 0, 0, tiled=True, axis_index_groups=across())
    image_own, *lows, sums = local(
        add_kernel, (f32(pairs, width),) + (b16(pairs + 16, width),) * 3 + (f32(8, 128),),
        image_own, *image_parts, spread,
    )
    image_parts = [send(p, along_first(-k), "rfirst") for p, k in zip(lows, OFFSETS)]
    text_own, far_low = local(
        far_kernel, (f32(pairs, width), b16(pairs, width)), text_own, text_far, back, after=(image_own,),
    )
    image_grad, text_grad, loss, bias_grad, temp_grad = local(
        finish_kernel, (f32(pairs, width),) * 2 + (f32(1),) * 3,
        log_temp, image_raw, image_own, *image_parts, text_raw, text_own, send(far_low, swap, "rpair"), sums,
    )
    return (loss, image_grad, text_grad, temp_grad, bias_grad)


def solution(mesh):
    fine = Mesh(mesh.devices.reshape(SIZES), AXES)
    rows = P(AXES, None)
    return jax.shard_map(
        body,
        mesh=fine,
        in_specs=(rows, rows, P(), P(), P(), P()),
        out_specs=(P(), rows, rows, P(), P()),
        check_vma=False,
    )
```
